128 devices in a mesh: ctx: 16 (over z, x_lo, core), head: 8 (over x_hi, y).
Axes of the slice: x: 4 (x_hi: 2, x_lo: 2; x = x_hi * 2 + x_lo), y: 4, z: 4, core: 2. Of those that a mesh axis runs over, the one named last changes fastest.
Arguments:
- block_order: int32 [32], replicated, may hold values from 0 to 31, each once
- question_lengths: int32 [16, 2], P('ctx'), may hold values from 32 to 96, as said below
- document_query_matrix: bfloat16 [2048, 12288], P('ctx', 'head'), may hold values from -6 to 6
- document_key_matrix: bfloat16 [2048, 1024], P('ctx', 'head'), may hold values from -6 to 6
- document_value_matrix: bfloat16 [2048, 1024], P('ctx', 'head'), may hold values from -6 to 6
- document_output: bfloat16 [2048, 12288], P('ctx', 'head'), may hold values from -6 to 6
- document_outgrad: bfloat16 [2048, 12288], P('ctx', 'head'), may hold values from -6 to 6
- document_excess: float32 [2048, 96], P('ctx', 'head'), may hold values from 0.2 to 1
- question_query_matrix: bfloat16 [2048, 12288], P(('ctx', 'head')), may hold values from -6 to 6
- question_key_matrix: bfloat16 [2048, 1024], P(('ctx', 'head')), may hold values from -6 to 6
- question_value_matrix: bfloat16 [2048, 1024], P(('ctx', 'head')), may hold values from -6 to 6
- question_output: bfloat16 [2048, 12288], P(('ctx', 'head')), may hold values from -6 to 6
- question_outgrad: bfloat16 [2048, 12288], P(('ctx', 'head')), may hold values from -6 to 6
- question_excess: float32 [2048, 96], P(('ctx', 'head')), may hold values from 0.2 to 1
Outputs:
- document_query_grad: bfloat16 [2048, 12288], P('ctx', 'head')
- document_keys_grad: bfloat16 [2048, 1024], P('ctx', 'head')
- document_values_grad: bfloat16 [2048, 1024], P('ctx', 'head')
- question_query_grad: bfloat16 [2048, 12288], P(('ctx', 'head'))
- question_keys_grad: bfloat16 [2048, 1024], P(('ctx', 'head'))
- question_values_grad: bfloat16 [2048, 1024], P(('ctx', 'head'))
The draws below stay inside these ranges and needn't reach their ends.
Inputs may be any that keep to these rules, and one draw needn't show every extreme that they name: `block_order`: a permutation: every block of 64 document positions is stored in exactly one slot; slots 2 c and 2 c + 1 lie on ctx index c. `question_lengths`: each row holds the lengths of the 2 questions of one group in packing order; they sum to 128; some group has a question of exactly 96 tokens.
All inputs are finite; a program needn't handle non-finite values.
Results may differ from the reference program's by a relative error of at most 0.007.
Values may be sent and summed in bfloat16 or wider, within the bound.
No kernel may reach another device: no remote copies, remote signals or barrier semaphores. Data moves between devices by JAX's collectives and lax.ppermute only.
A program may use at most 128 MiB of HBM per device.

```python
import jax
import jax.numpy as jnp
from jax import lax

QUERY_HEADS = 96
KEY_VALUE_HEADS = 8
HEAD_SIZE = 128
DOCUMENT_SHARE = 128
HALF = 64
DOCUMENT_LENGTH = 2048
GROUP_QUESTIONS = 128
QMAX = 96
QUESTION_TOKENS = 2048
N_CTX = 16


def draw_question_lengths(key, part):
    key = jax.random.fold_in(key, 7)
    first_key, pick_key, flip_key = jax.random.split(key, 3)
    longer = jax.random.randint(first_key, (N_CTX,), GROUP_QUESTIONS - QMAX, QMAX + 1)
    chosen = jax.random.randint(pick_key, (), 0, N_CTX)
    longer = jnp.where(jnp.arange(N_CTX) == chosen, QMAX, longer)
    flip = jax.random.randint(flip_key, (N_CTX,), 0, 2)
    leading = jnp.where(flip == 1, longer, GROUP_QUESTIONS - longer)
    return jnp.stack([leading, GROUP_QUESTIONS - leading], axis=1).astype(jnp.int32)


def levels(own_key, dims, shards, least, largest):
    factor_of = 1.0
    for axis_at, blocks in shards:
        steps = jax.random.uniform(jax.random.fold_in(jax.random.fold_in(own_key, 6), axis_at), (blocks,), jnp.float32, least / len(shards), largest / len(shards))
        factor_of = factor_of * jnp.repeat(jnp.exp(steps), dims[axis_at] // blocks).reshape((-1,) + (1,) * (len(dims) - 1 - axis_at))
    return factor_of


def normal_values(key, shape, scale, most, shards=(), kind=jnp.bfloat16):
    values = jax.random.normal(key, shape, jnp.float32) * scale
    if len(shards) > 0:
        values = levels(key, shape, shards, -0.22, 0.18) * values
    return jnp.clip(values, min=-most, max=most).astype(kind)


def setup_inputs(seed: int = 0) -> dict:
    splits = jax.random.split(jax.random.key(seed), 15)
    return {
        "block_order": jax.random.permutation(splits[0], 2 * N_CTX).astype(jnp.int32),
        "question_lengths": draw_question_lengths(jax.random.fold_in(splits[14], 71), 0),
        "document_query_matrix": normal_values(splits[2], (DOCUMENT_LENGTH, QUERY_HEADS * HEAD_SIZE), 1.0, 6.0, ((0, 16), (1, 8))),
        "document_key_matrix": normal_values(splits[3], (DOCUMENT_LENGTH, KEY_VALUE_HEADS * HEAD_SIZE), 1.0, 6.0, ((0, 16), (1, 8))),
        "document_value_matrix": normal_values(splits[4], (DOCUMENT_LENGTH, KEY_VALUE_HEADS * HEAD_SIZE), 1.0, 6.0, ((0, 16), (1, 8))),
        "document_output": normal_values(splits[5], (DOCUMENT_LENGTH, QUERY_HEADS * HEAD_SIZE), 1.0, 6.0, ((0, 16), (1, 8))),
        "document_outgrad": normal_values(splits[6], (DOCUMENT_LENGTH, QUERY_HEADS * HEAD_SIZE), 1.0, 6.0, ((0, 16), (1, 8))),
        "document_excess": jnp.clip(0.2 + 0.8 * jax.random.uniform(splits[7], (DOCUMENT_LENGTH, QUERY_HEADS), jnp.float32) ** levels(splits[7], (DOCUMENT_LENGTH, QUERY_HEADS), ((0, 16), (1, 8)), -0.2, 0.2), 0.2, 1.0),
        "question_query_matrix": normal_values(splits[8], (QUESTION_TOKENS, QUERY_HEADS * HEAD_SIZE), 1.0, 6.0, ((0, 128),)),
        "question_key_matrix": normal_values(splits[9], (QUESTION_TOKENS, KEY_VALUE_HEADS * HEAD_SIZE), 1.0, 6.0, ((0, 128),)),
        "question_value_matrix": normal_values(splits[10], (QUESTION_TOKENS, KEY_VALUE_HEADS * HEAD_SIZE), 1.0, 6.0, ((0, 128),)),
        "question_output": normal_values(splits[11], (QUESTION_TOKENS, QUERY_HEADS * HEAD_SIZE), 1.0, 6.0, ((0, 128),)),
        "question_outgrad": normal_values(splits[12], (QUESTION_TOKENS, QUERY_HEADS * HEAD_SIZE), 1.0, 6.0, ((0, 128),)),
        "question_excess": jnp.clip(0.2 + 0.8 * jax.random.uniform(splits[13], (QUESTION_TOKENS, QUERY_HEADS), jnp.float32) ** levels(splits[13], (QUESTION_TOKENS, QUERY_HEADS), ((0, 128),), -0.2, 0.2), 0.2, 1.0),
    }


def stored_positions(block_order, first_row, count, half):
    rows = first_row + jnp.arange(count, dtype=jnp.int32)
    blocks = jnp.arange(block_order.shape[0], dtype=jnp.int32)
    picked = (rows // half)[:, None] == blocks[None, :]
    owner = jnp.sum(jnp.where(picked, block_order[None, :], 0), axis=1).astype(jnp.int32)
    return owner * half + rows % half


def question_layout(lengths, count):
    ends = jnp.cumsum(lengths).astype(jnp.int32)
    starts = ends - lengths
    rows = jnp.arange(count, dtype=jnp.int32)
    segment = jnp.sum((rows[:, None] >= ends[None, :]).astype(jnp.int32), axis=1)
    member = segment[:, None] == jnp.arange(lengths.shape[0], dtype=jnp.int32)[None, :]
    within = rows - jnp.sum(jnp.where(member, starts[None, :], 0), axis=1).astype(jnp.int32)
    return segment, within


def delta_per_head(output, outgrad, heads):
    product = output.astype(jnp.float32) * outgrad.astype(jnp.float32)
    return jnp.sum(product.reshape(output.shape[0], heads, -1), axis=2)


def arrange_rows(values, kv_heads):
    return values.reshape(values.shape[0], kv_heads, -1).transpose(1, 2, 0)


def attend_block(query, outgrad, lse, delta, keys, values, mask):
    scale = query.shape[-1] ** -0.5
    query_f = query.astype(jnp.float32)
    grad_f = outgrad.astype(jnp.float32)
    keys_f = keys.astype(jnp.float32)
    values_f = values.astype(jnp.float32)
    scores = jnp.einsum('rkgd,nkd->kgrn', query_f, keys_f) * scale
    prob = jnp.exp(scores - lse[..., None])
    if mask is not None:
        prob = jnp.where(mask[None, None], prob, 0.0)
    prob_b = prob.astype(jnp.bfloat16).astype(jnp.float32)
    value_grad = jnp.einsum('kgrn,rkgd->nkd', prob_b, grad_f)
    dprob = jnp.einsum('rkgd,nkd->kgrn', grad_f, values_f)
    dscore = (prob * (dprob - delta[..., None])).astype(jnp.bfloat16).astype(jnp.float32)
    query_grad = jnp.einsum('kgrn,nkd->rkgd', dscore, keys_f) * scale
    key_grad = jnp.einsum('kgrn,rkgd->nkd', dscore, query_f) * scale
    return query_grad, key_grad, value_grad


def reference(block_order, question_lengths, document_query_matrix, document_key_matrix, document_value_matrix, document_output, document_outgrad, document_excess, question_query_matrix, question_key_matrix, question_value_matrix, question_output, question_outgrad, question_excess):
    document_key_rows = document_key_matrix.reshape(DOCUMENT_LENGTH, KEY_VALUE_HEADS, HEAD_SIZE)
    document_value_rows = document_value_matrix.reshape(DOCUMENT_LENGTH, KEY_VALUE_HEADS, HEAD_SIZE)
    key_pos = stored_positions(block_order, 0, DOCUMENT_LENGTH, HALF)

    def one_group(carry, group):
        key_acc, value_acc = carry
        start_index = (group * DOCUMENT_SHARE).astype(jnp.int32)
        query_row_block = lax.dynamic_slice_in_dim(document_query_matrix, start_index, DOCUMENT_SHARE, 0).reshape(DOCUMENT_SHARE, KEY_VALUE_HEADS, -1, HEAD_SIZE)
        gradient_rows = lax.dynamic_slice_in_dim(document_outgrad, start_index, DOCUMENT_SHARE, 0)
        output_rows = lax.dynamic_slice_in_dim(document_output, start_index, DOCUMENT_SHARE, 0)
        excess_row_block = lax.dynamic_slice_in_dim(document_excess, start_index, DOCUMENT_SHARE, 0)
        query_pos = stored_positions(block_order, start_index, DOCUMENT_SHARE, HALF)
        token_counts = (query_pos + 1).astype(jnp.float32)
        document_logsumexp = arrange_rows(excess_row_block + jnp.log(token_counts)[:, None], KEY_VALUE_HEADS)
        document_delta = arrange_rows(delta_per_head(output_rows, gradient_rows, QUERY_HEADS), KEY_VALUE_HEADS)
        document_mask = key_pos[None, :] <= query_pos[:, None]
        document_query_gradient, single_key_gradient, single_value_gradient = attend_block(query_row_block, gradient_rows.reshape(DOCUMENT_SHARE, KEY_VALUE_HEADS, -1, HEAD_SIZE), document_logsumexp, document_delta, document_key_rows, document_value_rows, document_mask)

        question_start = (group * GROUP_QUESTIONS).astype(jnp.int32)
        asked_rows = lax.dynamic_slice_in_dim(question_query_matrix, question_start, GROUP_QUESTIONS, 0).reshape(GROUP_QUESTIONS, KEY_VALUE_HEADS, -1, HEAD_SIZE)
        asked_gradient = lax.dynamic_slice_in_dim(question_outgrad, question_start, GROUP_QUESTIONS, 0)
        asked_output_rows = lax.dynamic_slice_in_dim(question_output, question_start, GROUP_QUESTIONS, 0)
        asked_excess_rows = lax.dynamic_slice_in_dim(question_excess, question_start, GROUP_QUESTIONS, 0)
        asked_key_rows = lax.dynamic_slice_in_dim(question_key_matrix, question_start, GROUP_QUESTIONS, 0).reshape(GROUP_QUESTIONS, KEY_VALUE_HEADS, HEAD_SIZE)
        asked_value_rows = lax.dynamic_slice_in_dim(question_value_matrix, question_start, GROUP_QUESTIONS, 0).reshape(GROUP_QUESTIONS, KEY_VALUE_HEADS, HEAD_SIZE)
        lengths = lax.dynamic_index_in_dim(question_lengths, group, 0, keepdims=False)
        segment, within = question_layout(lengths, GROUP_QUESTIONS)
        question_counts = (within + 1 + DOCUMENT_LENGTH).astype(jnp.float32)
        question_logsumexp = arrange_rows(asked_excess_rows + jnp.log(question_counts)[:, None], KEY_VALUE_HEADS)
        question_delta = arrange_rows(delta_per_head(asked_output_rows, asked_gradient, QUERY_HEADS), KEY_VALUE_HEADS)
        gradient4 = asked_gradient.reshape(GROUP_QUESTIONS, KEY_VALUE_HEADS, -1, HEAD_SIZE)
        dq_far, dk_two, dv_two = attend_block(asked_rows, gradient4, question_logsumexp, question_delta, document_key_rows, document_value_rows, None)
        self_mask = (segment[:, None] == segment[None, :]) & (within[None, :] <= within[:, None])
        dq_self, dk_self, dv_self = attend_block(asked_rows, gradient4, question_logsumexp, question_delta, asked_key_rows, asked_value_rows, self_mask)
        carry = (key_acc + single_key_gradient + dk_two, value_acc + single_value_gradient + dv_two)
        outputs = (document_query_gradient.astype(jnp.bfloat16).reshape(DOCUMENT_SHARE, -1),
                   (dq_far + dq_self).astype(jnp.bfloat16).reshape(GROUP_QUESTIONS, -1),
                   dk_self.astype(jnp.bfloat16).reshape(GROUP_QUESTIONS, -1),
                   dv_self.astype(jnp.bfloat16).reshape(GROUP_QUESTIONS, -1))
        return carry, outputs

    zero_filled = jnp.zeros((DOCUMENT_LENGTH, KEY_VALUE_HEADS, HEAD_SIZE), jnp.float32)
    (key_acc, value_acc), (document_query_gradient, dq_ques, dk_ques, dv_ques) = lax.scan(one_group, (zero_filled, zero_filled), jnp.arange(N_CTX, dtype=jnp.int32))
    return (document_query_gradient.reshape(DOCUMENT_LENGTH, -1),
            key_acc.astype(jnp.bfloat16).reshape(DOCUMENT_LENGTH, -1),
            value_acc.astype(jnp.bfloat16).reshape(DOCUMENT_LENGTH, -1),
            dq_ques.reshape(QUESTION_TOKENS, -1),
            dk_ques.reshape(QUESTION_TOKENS, -1),
            dv_ques.reshape(QUESTION_TOKENS, -1))
```

```python
import functools

import jax
import jax.numpy as jnp
from jax import lax
from jax.experimental import pallas as pl
from jax.experimental.pallas import tpu as pltpu
from jax.sharding import PartitionSpec as P

D = 128
SCALE = D**-0.5
LOG2E = 1.4426950408889634
HIDDEN = 1e30
BF = jnp.bfloat16
F32 = jnp.float32
VMEM = pltpu.CompilerParams(vmem_limit_bytes=40 * 2**20)


def dot(a, b, ca, cb):
    return lax.dot_general(a, b, (((ca,), (cb,)), ((), ())), preferred_element_type=F32)


def lanes(shape):
    return lax.broadcasted_iota(jnp.int32, shape, 1)


def sublanes(shape):
    return lax.broadcasted_iota(jnp.int32, shape, 0)


def smem():
    return pl.BlockSpec(memory_space=pltpu.SMEM)


def vmem():
    return pl.BlockSpec(memory_space=pltpu.VMEM)


def call(body, outs, n_smem, *args, **kw):
    return pl.pallas_call(
        body,
        out_shape=tuple(jax.ShapeDtypeStruct(s, t) for s, t in outs),
        in_specs=[smem()] * n_smem + [vmem()] * (len(args) - n_smem),
        out_specs=tuple(vmem() for _ in outs),
        compiler_params=VMEM,
        **kw,
    )(*args)


def pair_block(qs_ref, dos_ref, keys, values, lse, delta, mask):
    scores = dot(keys, qs_ref[...], 1, 1)
    dprob = dot(values, dos_ref[...], 1, 1)
    prob = jnp.exp2(scores * (SCALE * LOG2E) - lse)
    if mask is not None:
        prob = jnp.where(mask, prob, 0.0)
    dscore = (prob * (dprob - delta)).astype(BF)
    dv = dot(prob.astype(BF), dos_ref[...], 1, 0)
    dk = dot(dscore, qs_ref[...], 1, 0) * SCALE
    dq = dot(keys, dscore, 0, 0)
    return dq, dk, dv


def stack_heads(source, target, heads, first):
    for j in range(heads):
        at = first + j * D
        target[j * D : (j + 1) * D, :] = source[:, at : at + D]


def spread_rows(rows, target, heads):
    for j in range(heads):
        target[:, j * D : (j + 1) * D] = rows[j : j + 1, :]


def unstack_query_grad(dq, heads):
    return [(dq[:, j * D : (j + 1) * D].T * SCALE).astype(BF) for j in range(heads)]


def pack_kernel(heads, groups, total, len_ref, me_ref, q_ref, k_ref, v_ref, o_ref, do_ref, ex_ref, dk_ref, dv_ref, pay_ref, kv_ref, buf):
    rows = q_ref.shape[0]
    wide = heads * D
    kv_ref[:, :D] = dk_ref[...]
    kv_ref[:, D:] = dv_ref[...]
    row = me_ref[1] * rows + sublanes((rows, D))
    within = jnp.where(row < len_ref[0, 0], row, row - len_ref[0, 0])
    log_count = jnp.log((within + 1 + total).astype(F32))
    buf[:, : heads * groups] = ex_ref[...]
    lse = (buf[...] + log_count) * LOG2E
    lane = lanes((rows, D))
    for g in range(groups):
        delta = jnp.zeros((rows, D), F32)
        for j in range(heads):
            at = g * wide + j * D
            product = o_ref[:, at : at + D].astype(F32) * do_ref[:, at : at + D].astype(F32)
            delta = jnp.where(lane == j, jnp.sum(product, axis=1, keepdims=True), delta)
        mine = lse if g == 0 else pltpu.roll(lse, D - heads * g, 1)
        mine = jnp.where(lane < heads, mine, 0.0)
        stats = jnp.zeros((rows, D), F32)
        for n, value in enumerate((mine, delta)):
            for m in range(3):
                part = value.astype(BF).astype(F32)
                value = value - part
                at = (3 * n + m) * 16
                stats = stats + (pltpu.roll(part, at, 1) if at else part)
        pay_ref[g, :, :wide] = q_ref[:, g * wide : (g + 1) * wide]
        pay_ref[g, :, wide : 2 * wide] = do_ref[:, g * wide : (g + 1) * wide]
        pay_ref[g, :, 2 * wide : 2 * wide + D] = k_ref[:, g * D : (g + 1) * D]
        pay_ref[g, :, 2 * wide + D : 2 * wide + 2 * D] = v_ref[:, g * D : (g + 1) * D]
        pay_ref[g, :, 2 * wide + 2 * D :] = stats.astype(BF)


def doc_keys(order_ref, me, ctx_size, piece):
    core, z = piece
    place, low, step = me // 4, (me // 2) % 2, ctx_size // 4
    depth = lax.rem(place + step - z, step)
    return [(depth * 2 + (low ^ x if isinstance(low, int) else lax.bitwise_xor(low, x))) * 2 + lax.bitwise_xor(lax.rem(me, 2), core) for x in range(2)]


def doc_lse(order_ref, me, owner, lse, lane_half):
    parts = []
    for b in range(2):
        kb = order_ref[2 * owner + b]
        bias = [jnp.where(kb <= order_ref[2 * me + a], 0.0, HIDDEN).astype(F32) for a in range(2)]
        hide = jnp.where(lane_half, bias[1], bias[0])
        parts.append(jnp.broadcast_to(lse + hide, (D // 2, lse.shape[1])))
    return jnp.concatenate(parts, axis=0)


def doc_kernel(pieces, first, last, heads, ctx_size, order_ref, me_ref, *refs):
    n = len(pieces)
    refs = list(refs)
    kv_refs, refs = refs[:n], refs[n:]
    if first:
        q_ref, o_ref, do_ref, ex_ref = refs[:4]
        refs = refs[4:]
    else:
        qs_ref, dos_ref, lse_ref, delta_ref, dq_in = refs[:5]
        refs = refs[5:]
    if last:
        dq_out, refs = refs[0], refs[1:]
    out_refs, refs = refs[:n], refs[n:]
    if first and not last:
        dq_out, refs = refs[0], refs[1:]
    me = me_ref[0]
    rows = heads * D
    lane = lax.rem(lanes((1, rows)), D)
    half = D // 2
    lane_half = lane >= half
    if first:
        qs_ref, dos_ref, lse_ref, delta_ref = refs
        stack_heads(q_ref, qs_ref, heads, 0)
        stack_heads(do_ref, dos_ref, heads, 0)
        at = lanes((D, D))
        stats = jnp.zeros((D, D), F32)
        for j in range(heads):
            stats = jnp.where(at == j, ex_ref[:, j : j + 1], stats)
            cut = slice(j * D, (j + 1) * D)
            product = o_ref[:, cut].astype(F32) * do_ref[:, cut].astype(F32)
            stats = jnp.where(at == 16 + j, jnp.sum(product, axis=1, keepdims=True), stats)
        stats = stats.T
        one = lanes((1, D))
        pos = jnp.where(one < half, order_ref[2 * me] * half + one, order_ref[2 * me + 1] * half + one - half)
        spread_rows((stats[:16] + jnp.log((pos + 1).astype(F32))) * LOG2E, lse_ref, heads)
        spread_rows(stats[16:32], delta_ref, heads)
    lse = lse_ref[...]
    delta = delta_ref[...]
    total = None if first else dq_in[...]
    for n, piece in enumerate(pieces):
        owners = doc_keys(order_ref, me, ctx_size, piece)
        shift = jnp.concatenate([doc_lse(order_ref, me, o, lse, lane_half) for o in owners], axis=0)
        mask = None
        if piece == (0, 0):
            key = sublanes((2 * D, 1))
            own = key < D
            key_pos = jnp.where(key < half, order_ref[2 * me] * half + key, order_ref[2 * me + 1] * half + key - half)
            row_pos = jnp.where(lane_half, order_ref[2 * me + 1] * half + lane - half, order_ref[2 * me] * half + lane)
            mask = jnp.where(own, key_pos, -1) <= row_pos
        dq, dk, dv = pair_block(qs_ref, dos_ref, kv_refs[n][:, :D], kv_refs[n][:, D:], shift, delta, mask)
        out_refs[n][:, :D] = dk
        out_refs[n][:, D:] = dv
        total = dq if total is None else total + dq
    if last:
        for j, part in enumerate(unstack_query_grad(total, heads)):
            dq_out[:, j * D : (j + 1) * D] = part
    else:
        dq_out[...] = total


def far_kernel(heads, pay_ref, *refs):
    kv_refs, doc_refs = refs[:4], refs[4:8]
    send_ref, dq_ref, qs_ref, dos_ref, lse_ref, delta_ref = refs[8:]
    wide = heads * D
    stack_heads(pay_ref, qs_ref, heads, 0)
    stack_heads(pay_ref, dos_ref, heads, wide)
    stats = pay_ref[:, 2 * wide + 2 * D :].astype(F32).T
    spread_rows(stats[:16] + stats[16:32] + stats[32:48], lse_ref, heads)
    spread_rows(stats[48:64] + stats[64:80] + stats[80:96], delta_ref, heads)
    lse, delta = lse_ref[...], delta_ref[...]
    total = None
    for n in range(4):
        dq, dk, dv = pair_block(qs_ref, dos_ref, kv_refs[n][:, :D], kv_refs[n][:, D:], lse, delta, None)
        send_ref[n, :, :D] = (dk + doc_refs[n][:, :D]).astype(BF)
        send_ref[n, :, D:] = (dv + doc_refs[n][:, D:]).astype(BF)
        total = dq if total is None else total + dq
    dq_ref[...] = total


def near_kernel(heads, qs_ref, dos_ref, lse_ref, delta_ref, dq_in, *refs):
    kv_refs, doc_refs = refs[:4], refs[4:8]
    out_ref, dq_ref = refs[8:]
    lse, delta = lse_ref[...], delta_ref[...]
    total = dq_in[...]
    for pair in range(2):
        keys = jnp.concatenate([kv_refs[2 * pair + m][D:, :D] for m in range(2)], axis=0)
        values = jnp.concatenate([kv_refs[2 * pair + m][D:, D:] for m in range(2)], axis=0)
        dq, dk, dv = pair_block(qs_ref, dos_ref, keys, values, lse, delta, None)
        for m in range(2):
            n = 2 * pair + m
            out_ref[n, :, :D] = dk[m * D : (m + 1) * D] + doc_refs[n][D:, :D]
            out_ref[n, :, D:] = dv[m * D : (m + 1) * D] + doc_refs[n][D:, D:]
        total = total + dq
    dq_ref[...] = total


def own_kernel(heads, groups, len_ref, qs_ref, dos_ref, lse_ref, delta_ref, dq_in, pay_ref, *refs):
    kv_refs, doc_refs = refs[:4], refs[4:8]
    out_ref, back_ref = refs[8:]
    wide = heads * D
    lse, delta = lse_ref[...], delta_ref[...]
    rows = heads * D
    row = lax.rem(lanes((1, rows)), D)
    key = sublanes((D, 1))
    first = len_ref[0, 0]
    mask = (key <= row) & ((key >= first) | (row < first))
    keys = pay_ref[:, 2 * wide : 2 * wide + D]
    values = pay_ref[:, 2 * wide + D : 2 * wide + 2 * D]
    dq, dk, dv = pair_block(qs_ref, dos_ref, keys, values, lse, delta, mask)
    total = dq_in[...] + dq
    each = D // groups
    for g in range(groups):
        back_ref[g, :, wide : wide + D] = dk[g * each : (g + 1) * each].astype(BF)
        back_ref[g, :, wide + D :] = dv[g * each : (g + 1) * each].astype(BF)
    for pair in range(2):
        keys = jnp.concatenate([kv_refs[2 * pair + m][:D, :D] for m in range(2)], axis=0)
        values = jnp.concatenate([kv_refs[2 * pair + m][:D, D:] for m in range(2)], axis=0)
        dq, dk, dv = pair_block(qs_ref, dos_ref, keys, values, lse, delta, None)
        for m in range(2):
            n = 2 * pair + m
            out_ref[n, :, :D] = dk[m * D : (m + 1) * D] + doc_refs[n][:D, :D]
            out_ref[n, :, D:] = dv[m * D : (m + 1) * D] + doc_refs[n][:D, D:]
        total = total + dq
    for j, part in enumerate(unstack_query_grad(total, heads)):
        for g in range(groups):
            back_ref[g, :, j * D : (j + 1) * D] = part[g * each : (g + 1) * each]


def unpack_kernel(heads, groups, back_ref, q_ref, k_ref, v_ref):
    wide = heads * D
    for g in range(groups):
        q_ref[:, g * wide : (g + 1) * wide] = back_ref[g, :, :wide]
        k_ref[:, g * D : (g + 1) * D] = back_ref[g, :, wide : wide + D]
        v_ref[:, g * D : (g + 1) * D] = back_ref[g, :, wide + D :]


def local(
    block_order,
    question_lengths,
    document_query_matrix,
    document_key_matrix,
    document_value_matrix,
    document_output,
    document_outgrad,
    document_excess,
    question_query_matrix,
    question_key_matrix,
    question_value_matrix,
    question_output,
    question_outgrad,
    question_excess,
):
    ctx_size, groups = lax.axis_size("ctx"), lax.axis_size("head")
    heads = document_excess.shape[1]
    rows, each = document_query_matrix.shape[0], question_query_matrix.shape[0]
    total_doc = rows * ctx_size
    wide, stacked = heads * D, heads * rows
    me = jnp.stack([lax.axis_index("ctx"), lax.axis_index("head")]).astype(jnp.int32)
    depth = ctx_size // 4

    def other_core(x):
        return lax.ppermute(x, "ctx", [(i, i ^ 1) for i in range(ctx_size)])

    def other_chip(x):
        return lax.ppermute(x, "ctx", [(i, i ^ 2) for i in range(ctx_size)])

    def along_z(x, d):
        return lax.ppermute(x, "ctx", [(i, (i + 4 * d) % ctx_size) for i in range(ctx_size)])

    payload, kv = call(
        functools.partial(pack_kernel, heads, groups, total_doc),
        [((groups, each, 2 * wide + 3 * D), BF), ((rows, 2 * D), BF)],
        2,
        question_lengths, me, question_query_matrix, question_key_matrix, question_value_matrix, question_output,
        question_outgrad, question_excess, document_key_matrix, document_value_matrix,
        scratch_shapes=[pltpu.VMEM((each, D), F32)],
    )
    asked = lax.all_to_all(payload, "head", 0, 0, tiled=True).reshape(groups * each, -1)
    here = jnp.concatenate([kv, other_chip(kv)], axis=0)
    mine = [here] + [along_z(here, d) for d in range(1, depth)]
    theirs = [other_core(piece) for piece in mine]

    piece_grad = ((2 * rows, 2 * D), F32)
    row_state = [((stacked, D), BF), ((stacked, D), BF), ((1, stacked), F32), ((1, stacked), F32)]
    early = ((0, 0), (1, 0))
    late = tuple((0, d) for d in range(1, depth)) + tuple((1, d) for d in range(1, depth))
    first = call(
        functools.partial(doc_kernel, early, True, False, heads, ctx_size),
        [piece_grad] * 2 + [((D, stacked), F32)] + row_state,
        2,
        block_order, me, mine[0], theirs[0], document_query_matrix, document_output, document_outgrad, document_excess,
    )
    second = call(
        functools.partial(doc_kernel, late, False, True, heads, ctx_size),
        [((rows, wide), BF)] + [piece_grad] * 6,
        2,
        block_order, me, *mine[1:], *theirs[1:], *first[3:], first[2],
    )
    document_query_grad = second[0]
    doc_mine = (first[0],) + tuple(second[1 : depth])
    doc_theirs = (first[1],) + tuple(second[depth:])

    far = call(
        functools.partial(far_kernel, heads),
        [((4, 2 * rows, 2 * D), BF), ((D, stacked), F32)] + row_state,
        0,
        asked, *theirs, *doc_theirs,
    )
    core_sum = other_core(far[0])
    near, dq_near = call(
        functools.partial(near_kernel, heads),
        [((4, rows, 2 * D), F32), ((D, stacked), F32)],
        0,
        *far[2:], far[1], *mine, *doc_mine,
    )
    chip_sum = other_chip((near + core_sum[:, rows:].astype(F32)).astype(BF))
    own, back = call(
        functools.partial(own_kernel, heads, groups),
        [((4, rows, 2 * D), F32), ((groups, each, wide + 2 * D), BF)],
        1,
        question_lengths, *far[2:], dq_near, asked, *mine, *doc_mine,
    )
    back = lax.all_to_all(back, "head", 0, 0, tiled=True)
    held = own + core_sum[:, :rows].astype(F32) + chip_sum.astype(F32)
    grads = held[0]
    for d in range(1, depth):
        grads = grads + along_z(held[d].astype(BF), depth - d).astype(F32)
    grads = grads.astype(BF)
    question_query_grad, question_keys_grad, question_values_grad = call(
        functools.partial(unpack_kernel, heads, groups),
        [((each, wide * groups), BF), ((each, D * groups), BF), ((each, D * groups), BF)],
        0,
        back,
    )
    return (
        document_query_grad,
        grads[:, :D],
        grads[:, D:],
        question_query_grad,
        question_keys_grad,
        question_values_grad,
    )


def solution(mesh):
    return jax.shard_map(
        local,
        mesh=mesh,
        in_specs=(
            P(),
            P("ctx", None),
            P("ctx", "head"),
            P("ctx", "head"),
            P("ctx", "head"),
            P("ctx", "head"),
            P("ctx", "head"),
            P("ctx", "head"),
            P(("ctx", "head"), None),
            P(("ctx", "head"), None),
            P(("ctx", "head"), None),
            P(("ctx", "head"), None),
            P(("ctx", "head"), None),
            P(("ctx", "head"), None),
        ),
        out_specs=(
            P("ctx", "head"),
            P("ctx", "head"),
            P("ctx", "head"),
            P(("ctx", "head"), None),
            P(("ctx", "head"), None),
            P(("ctx", "head"), None),
        ),
        check_vma=False,
    )
```

```python
import functools

import jax
import jax.numpy as jnp
from jax import lax
from jax.experimental import pallas as pl
from jax.experimental.pallas import tpu as pltpu
from jax.sharding import PartitionSpec as P

D = 128
SCALE = D**-0.5
LOG2E = 1.4426950408889634
HIDDEN = 1e30
BF = jnp.bfloat16
F32 = jnp.float32
SHARED = pltpu.CompilerParams(vmem_limit_bytes=20 * 2**20)
WHOLE = pltpu.CompilerParams(vmem_limit_bytes=60 * 2**20)


def dot(a, b, ca, cb):
    return lax.dot_general(a, b, (((ca,), (cb,)), ((), ())), preferred_element_type=F32)


def lanes(shape):
    return lax.broadcasted_iota(jnp.int32, shape, 1)


def sublanes(shape):
    return lax.broadcasted_iota(jnp.int32, shape, 0)


def smem():
    return pl.BlockSpec(memory_space=pltpu.SMEM)


def vmem():
    return pl.BlockSpec(memory_space=pltpu.VMEM)


def hbm():
    return pl.BlockSpec(memory_space=pltpu.HBM)


def cost(us):
    return pl.CostEstimate(flops=int(us * 1.1e9), bytes_accessed=0, transcendentals=0)


def call(us, body, outs, n_smem, *args, **kw):
    return pl.pallas_call(
        body,
        out_shape=tuple(jax.ShapeDtypeStruct(s, t) for s, t in outs),
        in_specs=[smem()] * n_smem + [vmem()] * (len(args) - n_smem),
        out_specs=tuple(vmem() for _ in outs),
        compiler_params=SHARED,
        cost_estimate=cost(us),
        **kw,
    )(*args)


def pair_block(qs_ref, dos_ref, keys, values, lse, delta, mask):
    scores = dot(keys, qs_ref[...], 1, 1)
    dprob = dot(values, dos_ref[...], 1, 1)
    prob = jnp.exp2(scores * (SCALE * LOG2E) - lse)
    if mask is not None:
        prob = jnp.where(mask, prob, 0.0)
    dscore = (prob * (dprob - delta)).astype(BF)
    dv = dot(prob.astype(BF), dos_ref[...], 1, 0)
    dk = dot(dscore, qs_ref[...], 1, 0) * SCALE
    dq = dot(keys, dscore, 0, 0)
    return dq, dk, dv


def both(ref):
    keys = jnp.concatenate([ref[:D], ref[2 * D : 3 * D]], axis=0)
    values = jnp.concatenate([ref[D : 2 * D], ref[3 * D :]], axis=0)
    return keys, values


def stack_heads(source, target, heads, first):
    for j in range(heads):
        at = first + j * D
        target[j * D : (j + 1) * D, :] = source[:, at : at + D]


def spread_rows(rows, target, heads):
    for j in range(heads):
        target[:, j * D : (j + 1) * D] = rows[j : j + 1, :]


def unstack_query_grad(dq, heads):
    return [(dq[:, j * D : (j + 1) * D].T * SCALE).astype(BF) for j in range(heads)]


def stats_kernel(heads, groups, total, len_ref, me_ref, o_ref, do_ref, ex_ref, packed, out, grad, buf, sems):
    rows = out.shape[0]
    wide = heads * D
    loads = [pltpu.make_async_copy(source, to, sems.at[n]) for n, (source, to) in enumerate(((o_ref, out), (do_ref, grad), (ex_ref, buf)))]
    for load in loads:
        load.start()
    row = me_ref[1] * rows + sublanes((rows, D))
    within = jnp.where(row < len_ref[0, 0], row, row - len_ref[0, 0])
    log_count = jnp.log((within + 1 + total).astype(F32))
    for load in loads:
        load.wait()
    lse = (buf[...] + log_count[:, : heads * groups]) * LOG2E
    lse = jnp.concatenate([lse, jnp.zeros((rows, D - heads * groups), F32)], axis=1)
    lane = lanes((rows, D))
    for g in range(groups):
        delta = jnp.zeros((rows, D), F32)
        for j in range(heads):
            cut = slice(g * wide + j * D, g * wide + (j + 1) * D)
            product = out[:, cut].astype(F32) * grad[:, cut].astype(F32)
            delta = jnp.where(lane == j, jnp.sum(product, axis=1, keepdims=True), delta)
        mine = lse if g == 0 else pltpu.roll(lse, D - heads * g, 1)
        mine = jnp.where(lane < heads, mine, 0.0)
        stats = jnp.zeros((rows, D), F32)
        for n, value in enumerate((mine, delta)):
            for m in range(3):
                part = value.astype(BF).astype(F32)
                value = value - part
                at = (3 * n + m) * 16
                stats = stats + (pltpu.roll(part, at, 1) if at else part)
        packed[g] = stats.astype(BF)


def pack_kernel(heads, groups, stats_ref, q_ref, do_ref, k_ref, v_ref, pay_ref, stats, query, grad, keys, values, sems):
    wide = heads * D
    pairs = ((q_ref, query), (do_ref, grad), (k_ref, keys), (v_ref, values), (stats_ref, stats))
    loads = [pltpu.make_async_copy(source, to, sems.at[n]) for n, (source, to) in enumerate(pairs)]
    for load in loads:
        load.start()
    sends = []
    for n, (source, to, size) in enumerate(((query, 0, wide), (grad, wide, wide), (keys, 2 * wide, D), (values, 2 * wide + D, D))):
        loads[n].wait()
        for g in range(groups):
            part = pay_ref.at[g, :, pl.ds(to, size)]
            sends.append(pltpu.make_async_copy(source.at[:, pl.ds(g * size, size)], part, sems.at[5 + n * groups + g]))
            sends[-1].start()
    loads[4].wait()
    sends.append(pltpu.make_async_copy(stats, pay_ref.at[:, :, pl.ds(2 * wide + 2 * D, D)], sems.at[5 + 4 * groups]))
    sends[-1].start()
    for copy in sends:
        copy.wait()


def doc_keys(order_ref, me, ctx_size, piece):
    core, z = piece
    place, low, step = me // 4, (me // 2) % 2, ctx_size // 4
    depth = lax.rem(place + step - z, step)
    return [(depth * 2 + (low ^ x if isinstance(low, int) else lax.bitwise_xor(low, x))) * 2 + lax.bitwise_xor(lax.rem(me, 2), core) for x in range(2)]


def doc_lse(order_ref, me, owner, lse, lane_half):
    parts = []
    for b in range(2):
        kb = order_ref[2 * owner + b]
        bias = [jnp.where(kb <= order_ref[2 * me + a], 0.0, HIDDEN).astype(F32) for a in range(2)]
        hide = jnp.where(lane_half, bias[1], bias[0])
        parts.append(jnp.broadcast_to(lse + hide, (D // 2, lse.shape[1])))
    return jnp.concatenate(parts, axis=0)


def doc_kernel(core, heads, ctx_size, order_ref, me_ref, *refs):
    kv_hbm, refs = refs[:4], refs[4:]
    kv_refs, sems = refs[-2:]
    if core == 0:
        ins, state_hbm, (dq_hbm, near_hbm, own_hbm) = refs[:4], refs[4:8], refs[8:11]
        bufs, state, (dq_ref, near_ref, own_ref) = refs[11:15], refs[15:19], refs[19:22]
        q_ref, o_ref, do_ref, ex_ref = bufs
    else:
        ins, (dq_hbm, far_hbm) = refs[:5], refs[5:7]
        bufs, (dq_ref, far_ref) = refs[7:12], refs[12:14]
        state = bufs[:4]
    qs_ref, dos_ref, lse_ref, delta_ref = state
    loads = [pltpu.make_async_copy(source, to, sems.at[n]) for n, (source, to) in enumerate(zip(ins, bufs))]
    pieces = [pltpu.make_async_copy(kv_hbm[n], kv_refs.at[n], sems.at[5 + n]) for n in range(4)]
    for load in loads[:4] + pieces + loads[4:]:
        load.start()
    stores = []

    def store(source, to):
        stores.append(pltpu.make_async_copy(source, to, sems.at[9 + len(stores)]))
        stores[-1].start()

    me = me_ref[0]
    rows = heads * D
    lane = lax.rem(lanes((1, rows)), D)
    half = D // 2
    lane_half = lane >= half
    if core == 0:
        loads[3].wait()
        one = lanes((1, D))
        pos = jnp.where(one < half, order_ref[2 * me] * half + one, order_ref[2 * me + 1] * half + one - half)
        spread_rows((ex_ref[...] + jnp.log((pos + 1).astype(F32))) * LOG2E, lse_ref, heads)
        loads[0].wait()
        stack_heads(q_ref, qs_ref, heads, 0)
        loads[2].wait()
        stack_heads(do_ref, dos_ref, heads, 0)
        loads[1].wait()
        at = lanes((D, D))
        stats = jnp.zeros((D, D), F32)
        for j in range(heads):
            cut = slice(j * D, (j + 1) * D)
            product = o_ref[:, cut].astype(F32) * do_ref[:, cut].astype(F32)
            stats = jnp.where(at == j, jnp.sum(product, axis=1, keepdims=True), stats)
        spread_rows(stats.T[:16], delta_ref, heads)
        for source, to in zip(state, state_hbm):
            store(source, to)
    else:
        for load in loads[:4]:
            load.wait()
    lse = lse_ref[...]
    delta = delta_ref[...]
    total = None
    for depth in range(4):
        owners = doc_keys(order_ref, me, ctx_size, (core, depth))
        shift = jnp.concatenate([doc_lse(order_ref, me, o, lse, lane_half) for o in owners], axis=0)
        mask = None
        if core == 0 and depth == 0:
            key = sublanes((2 * D, 1))
            key_pos = jnp.where(key < half, order_ref[2 * me] * half + key, order_ref[2 * me + 1] * half + key - half)
            row_pos = jnp.where(lane_half, order_ref[2 * me + 1] * half + lane - half, order_ref[2 * me] * half + lane)
            mask = jnp.where(key < D, key_pos, -1) <= row_pos
        pieces[depth].wait()
        dq, dk, dv = pair_block(qs_ref, dos_ref, *both(kv_refs.at[depth]), shift, delta, mask)
        for side, grad in enumerate((dk, dv)):
            cut = slice(side * D, (side + 1) * D)
            if core == 0:
                own_ref[depth, :, cut] = grad[:D]
                near_ref[depth, :, cut] = grad[D:]
            else:
                far_ref[depth, :, cut] = grad
        total = dq if total is None else total + dq
        if core == 0:
            store(own_ref.at[depth], own_hbm.at[depth])
            store(near_ref.at[depth], near_hbm.at[depth])
        else:
            store(far_ref.at[depth], far_hbm.at[depth])
    if core == 0:
        dq_ref[...] = total
    else:
        loads[4].wait()
        for j, part in enumerate(unstack_query_grad(total + bufs[4][...], heads)):
            dq_ref[:, j * D : (j + 1) * D] = part
    store(dq_ref, dq_hbm)
    for copy in stores:
        copy.wait()


def self_kernel(heads, len_ref, pay_ref, qs_ref, dos_ref, lse_ref, delta_ref, self_ref, dq_ref):
    wide = heads * D
    stack_heads(pay_ref, qs_ref, heads, 0)
    stack_heads(pay_ref, dos_ref, heads, wide)
    stats = pay_ref[:, 2 * wide + 2 * D :].astype(F32).T
    spread_rows(stats[:16] + stats[16:32] + stats[32:48], lse_ref, heads)
    spread_rows(stats[48:64] + stats[64:80] + stats[80:96], delta_ref, heads)
    row = lax.rem(lanes((1, wide)), D)
    key = sublanes((D, 1))
    first = len_ref[0, 0]
    mask = (key <= row) & ((key >= first) | (row < first))
    keys = pay_ref[:, 2 * wide : 2 * wide + D]
    values = pay_ref[:, 2 * wide + D : 2 * wide + 2 * D]
    dq, dk, dv = pair_block(qs_ref, dos_ref, keys, values, lse_ref[...], delta_ref[...], mask)
    self_ref[:, :D] = dk.astype(BF)
    self_ref[:, D:] = dv.astype(BF)
    dq_ref[...] = dq


def far_kernel(qs_ref, dos_ref, lse_ref, delta_ref, dq_in, *refs):
    kv_refs, doc_ref = refs[:4], refs[4]
    send_ref, dq_ref = refs[5:]
    lse, delta = lse_ref[...], delta_ref[...]
    total = dq_in[...]
    for n in range(4):
        dq, dk, dv = pair_block(qs_ref, dos_ref, *both(kv_refs[n]), lse, delta, None)
        send_ref[n, :, :D] = (dk + doc_ref[n, :, :D]).astype(BF)
        send_ref[n, :, D:] = (dv + doc_ref[n, :, D:]).astype(BF)
        total = total + dq
    dq_ref[...] = total


def column(x, qs_ref, dos_ref, lse, delta, kv_refs, total, store):
    for pair in range(len(kv_refs) // 2):
        refs = [kv_refs[2 * pair + m] for m in range(2)]
        keys = jnp.concatenate([ref[2 * x * D : 2 * x * D + D] for ref in refs], axis=0)
        values = jnp.concatenate([ref[2 * x * D + D : 2 * x * D + 2 * D] for ref in refs], axis=0)
        dq, dk, dv = pair_block(qs_ref, dos_ref, keys, values, lse, delta, None)
        for m in range(2):
            part = slice(m * D, (m + 1) * D)
            store(2 * pair + m, slice(0, D), dk[part])
            store(2 * pair + m, slice(D, 2 * D), dv[part])
        total = total + dq
    return total


def near_kernel(qs_ref, dos_ref, lse_ref, delta_ref, dq_in, core_ref, *refs):
    kv_refs, doc_ref = refs[:4], refs[4]
    send_ref, dq_ref = refs[5:]

    def store(n, cut, grad):
        send_ref[n, :, cut] = (grad + doc_ref[n, :, cut] + core_ref[n, D:, cut].astype(F32)).astype(BF)

    dq_ref[...] = column(1, qs_ref, dos_ref, lse_ref[...], delta_ref[...], kv_refs, dq_in[...], store)


def own_kernel(qs_ref, dos_ref, lse_ref, delta_ref, dq_in, *refs):
    kv_refs = refs[:2]
    out_ref, dq_ref = refs[2:]

    def store(n, cut, grad):
        out_ref[n, :, cut] = grad

    dq_ref[...] = column(0, qs_ref, dos_ref, lse_ref[...], delta_ref[...], kv_refs, dq_in[...], store)


def last_kernel(heads, groups, qs_ref, dos_ref, lse_ref, delta_ref, dq_in, self_ref, *refs):
    kv_refs = refs[:2]
    out_ref, back_ref = refs[2:]
    wide = heads * D

    def store(n, cut, grad):
        out_ref[n, :, cut] = grad

    total = column(0, qs_ref, dos_ref, lse_ref[...], delta_ref[...], kv_refs, dq_in[...], store)
    each = D // groups
    for g in range(groups):
        back_ref[g, :, wide:] = self_ref[g * each : (g + 1) * each]
    for j, part in enumerate(unstack_query_grad(total, heads)):
        for g in range(groups):
            back_ref[g, :, j * D : (j + 1) * D] = part[g * each : (g + 1) * each]


def held_kernel(low_ref, high_ref, doc_ref, core_ref, chip_ref, keep_ref, *send_refs):
    for n in range(4):
        own = low_ref[n] if n < 2 else high_ref[n - 2]
        held = own + doc_ref[n] + core_ref[n, :D].astype(F32) + chip_ref[n].astype(F32)
        if n == 0:
            keep_ref[...] = held
        else:
            send_refs[n - 1][...] = held.astype(BF)


def unpack_kernel(heads, groups, back_ref, keep_ref, *refs):
    q_ref, k_ref, v_ref, dk_ref, dv_ref = refs[3:]
    wide = heads * D
    total = keep_ref[...]
    for ref in refs[:3]:
        total = total + ref[...].astype(F32)
    dk_ref[...] = total[:, :D].astype(BF)
    dv_ref[...] = total[:, D:].astype(BF)
    for g in range(groups):
        q_ref[:, g * wide : (g + 1) * wide] = back_ref[g, :, :wide]
        k_ref[:, g * D : (g + 1) * D] = back_ref[g, :, wide : wide + D]
        v_ref[:, g * D : (g + 1) * D] = back_ref[g, :, wide + D :]


def local(
    block_order,
    question_lengths,
    document_query_matrix,
    document_key_matrix,
    document_value_matrix,
    document_output,
    document_outgrad,
    document_excess,
    question_query_matrix,
    question_key_matrix,
    question_value_matrix,
    question_output,
    question_outgrad,
    question_excess,
):
    ctx_size, groups = lax.axis_size("ctx"), lax.axis_size("head")
    heads = document_excess.shape[1]
    rows, each = document_query_matrix.shape[0], question_query_matrix.shape[0]
    total_doc = rows * ctx_size
    wide, stacked = heads * D, heads * rows
    me = jnp.stack([lax.axis_index("ctx"), lax.axis_index("head")]).astype(jnp.int32)
    depth = ctx_size // 4

    def other_core(x):
        return lax.ppermute(x, "ctx", [(i, i ^ 1) for i in range(ctx_size)])

    def other_chip(x):
        return lax.ppermute(x, "ctx", [(i, i ^ 2) for i in range(ctx_size)])

    def along_z(x, d):
        return lax.ppermute(x, "ctx", [(i, (i + 4 * d) % ctx_size) for i in range(ctx_size)])

    kv = jnp.concatenate([document_key_matrix, document_value_matrix], axis=0)
    here = jnp.concatenate([kv, other_chip(kv)], axis=0)
    mine = [here] + [along_z(here, d) for d in range(1, depth)]
    theirs = [other_core(piece) for piece in mine]
    def copying(us, body, outs, n_smem, scratch, *args):
        return pl.pallas_call(
            body,
            out_shape=tuple(jax.ShapeDtypeStruct(s, t) for s, t in outs),
            in_specs=[smem()] * n_smem + [hbm()] * (len(args) - n_smem),
            out_specs=(hbm(),) * len(outs),
            scratch_shapes=scratch,
            compiler_params=WHOLE,
            cost_estimate=cost(us),
        )(*args)

    asking = pltpu.VMEM((each, wide * groups), BF)
    parts = (groups, each, D)
    stats = pl.pallas_call(
        functools.partial(stats_kernel, heads, groups, total_doc),
        out_shape=jax.ShapeDtypeStruct(parts, BF),
        in_specs=[smem()] * 2 + [hbm()] * 3,
        out_specs=vmem(),
        scratch_shapes=[asking, asking, pltpu.VMEM((each, heads * groups), F32), pltpu.SemaphoreType.DMA((3,))],
        compiler_params=WHOLE,
        cost_estimate=cost(3),
    )(question_lengths, me, question_output, question_outgrad, question_excess)
    (payload,) = copying(
        4,
        functools.partial(pack_kernel, heads, groups),
        [((groups, each, 2 * wide + 3 * D), BF)],
        0,
        [pltpu.VMEM(parts, BF), asking, asking]
        + [pltpu.VMEM((each, D * groups), BF)] * 2
        + [pltpu.SemaphoreType.DMA((6 + 4 * groups,))],
        stats, question_query_matrix, question_outgrad, question_key_matrix, question_value_matrix,
    )
    asked = lax.all_to_all(payload, "head", 0, 0, tiled=True).reshape(groups * each, -1)

    quarter = ((depth, rows, 2 * D), F32)
    double = ((depth, 2 * rows, 2 * D), F32)
    row_state = [((stacked, D), BF), ((stacked, D), BF), ((1, stacked), F32), ((1, stacked), F32)]
    query_sum = ((D, stacked), F32)
    flat = ((rows, wide), BF)

    def held(*shapes):
        return [pltpu.VMEM(*shape) for shape in shapes] + [pltpu.VMEM((depth, 4 * rows, D), BF), pltpu.SemaphoreType.DMA((24,))]

    *doc_state, dq, near_doc, own_doc = copying(
        6,
        functools.partial(doc_kernel, 0, heads, ctx_size),
        row_state + [query_sum, quarter, quarter],
        2,
        held(flat, flat, flat, ((heads, rows), F32), *row_state, query_sum, quarter, quarter),
        block_order, me, *mine, document_query_matrix, document_output, document_outgrad, document_excess.T,
    )
    document_query_grad, far_doc = copying(
        6,
        functools.partial(doc_kernel, 1, heads, ctx_size),
        [flat, double],
        2,
        held(*row_state, query_sum, flat, double),
        block_order, me, *theirs, *doc_state, dq,
    )
    *state, own_self, dq = call(
        1.5,
        functools.partial(self_kernel, heads),
        row_state + [((rows, 2 * D), BF), query_sum],
        1,
        question_lengths, asked,
    )
    far, dq = call(4.4, far_kernel, [((depth, 2 * rows, 2 * D), BF), query_sum], 0, *state, dq, *theirs, far_doc)
    core_sum = other_core(far)
    low, dq = call(1.5, own_kernel, [((2, rows, 2 * D), F32), query_sum], 0, *state, dq, *mine[:2])
    near, dq = call(2.2, near_kernel, [((depth, rows, 2 * D), BF), query_sum], 0, *state, dq, core_sum, *mine, near_doc)
    chip_sum = other_chip(near)
    high, back = call(
        2,
        functools.partial(last_kernel, heads, groups),
        [((2, rows, 2 * D), F32), ((groups, each, wide + 2 * D), BF)],
        0,
        *state, dq, own_self, *mine[2:],
    )
    back = lax.all_to_all(back, "head", 0, 0, tiled=True)
    keep, *sends = call(
        25,
        held_kernel,
        [((rows, 2 * D), F32)] + [((rows, 2 * D), BF)] * (depth - 1),
        0,
        low, high, own_doc, core_sum, chip_sum,
    )
    arrived = [along_z(send, depth - 1 - n) for n, send in enumerate(sends)]
    question_query_grad, question_keys_grad, question_values_grad, document_keys_grad, document_values_grad = call(
        0.8,
        functools.partial(unpack_kernel, heads, groups),
        [((each, wide * groups), BF), ((each, D * groups), BF), ((each, D * groups), BF), ((rows, D), BF), ((rows, D), BF)],
        0,
        back, keep, *arrived,
    )
    return (
        document_query_grad,
        document_keys_grad,
        document_values_grad,
        question_query_grad,
        question_keys_grad,
        question_values_grad,
    )


def solution(mesh):
    return jax.shard_map(
        local,
        mesh=mesh,
        in_specs=(
            P(),
            P("ctx", None),
            P("ctx", "head"),
            P("ctx", "head"),
            P("ctx", "head"),
            P("ctx", "head"),
            P("ctx", "head"),
            P("ctx", "head"),
            P(("ctx", "head"), None),
            P(("ctx", "head"), None),
            P(("ctx", "head"), None),
            P(("ctx", "head"), None),
            P(("ctx", "head"), None),
            P(("ctx", "head"), None),
        ),
        out_specs=(
            P("ctx", "head"),
            P("ctx", "head"),
            P("ctx", "head"),
            P(("ctx", "head"), None),
            P(("ctx", "head"), None),
            P(("ctx", "head"), None),
        ),
        check_vma=False,
    )
```

```python
import functools

import jax
import jax.numpy as jnp
from jax import lax
from jax.experimental import pallas as pl
from jax.experimental.pallas import tpu as pltpu
from jax.sharding import PartitionSpec as P

D = 128
SCALE = D**-0.5
LOG2E = 1.4426950408889634
HIDDEN = 1e30
BF = jnp.bfloat16
F32 = jnp.float32
SHARED = pltpu.CompilerParams(vmem_limit_bytes=20 * 2**20)
WHOLE = pltpu.CompilerParams(vmem_limit_bytes=60 * 2**20)


def dot(a, b, ca, cb):
    return lax.dot_general(a, b, (((ca,), (cb,)), ((), ())), preferred_element_type=F32)


def lanes(shape):
    return lax.broadcasted_iota(jnp.int32, shape, 1)


def sublanes(shape):
    return lax.broadcasted_iota(jnp.int32, shape, 0)


def smem():
    return pl.BlockSpec(memory_space=pltpu.SMEM)


def vmem():
    return pl.BlockSpec(memory_space=pltpu.VMEM)


def hbm():
    return pl.BlockSpec(memory_space=pltpu.HBM)


def cost(us):
    return pl.CostEstimate(flops=int(us * 1.1e9), bytes_accessed=0, transcendentals=0)


def call(us, body, outs, n_smem, *args, **kw):
    return pl.pallas_call(
        body,
        out_shape=tuple(jax.ShapeDtypeStruct(s, t) for s, t in outs),
        in_specs=[smem()] * n_smem + [vmem()] * (len(args) - n_smem),
        out_specs=tuple(vmem() for _ in outs),
        compiler_params=SHARED,
        cost_estimate=cost(us),
        **kw,
    )(*args)


def pair_block(qs_ref, dos_ref, keys, values, lse, delta, mask):
    scores = dot(keys, qs_ref[...], 1, 1)
    dprob = dot(values, dos_ref[...], 1, 1)
    scores = scores * (SCALE * LOG2E)
    if isinstance(lse, list):
        step = scores.shape[0] // len(lse)
        prob = jnp.concatenate([jnp.exp2(scores[n * step : (n + 1) * step] - row) for n, row in enumerate(lse)], axis=0)
    else:
        prob = jnp.exp2(scores - lse)
    if mask is not None:
        prob = jnp.where(mask, prob, 0.0)
    dscore = (prob * (dprob - delta)).astype(BF)
    dv = dot(prob.astype(BF), dos_ref[...], 1, 0)
    dk = dot(dscore, qs_ref[...], 1, 0) * SCALE
    dq = dot(keys, dscore, 0, 0)
    return dq, dk, dv


def both(ref):
    keys = jnp.concatenate([ref[:D], ref[2 * D : 3 * D]], axis=0)
    values = jnp.concatenate([ref[D : 2 * D], ref[3 * D :]], axis=0)
    return keys, values


def head_parts(out, grad):
    product = out.astype(F32) * grad.astype(F32)
    high = product.astype(BF)
    return high, (product - high.astype(F32)).astype(BF)


def head_ones(shape, axis):
    position = lax.broadcasted_iota(jnp.int32, shape, 1 - axis) // D
    return jnp.where(position == lax.broadcasted_iota(jnp.int32, shape, axis), 1.0, 0.0).astype(BF)


def stack_heads(source, target, heads, first):
    for j in range(heads):
        at = first + j * D
        target[j * D : (j + 1) * D, :] = source[:, at : at + D]


def spread_rows(rows, target, heads):
    for j in range(heads):
        target[:, j * D : (j + 1) * D] = rows[j : j + 1, :]


def unstack_query_grad(dq, heads):
    dq = (dq * SCALE).astype(BF)
    return [dq[:, j * D : (j + 1) * D].T for j in range(heads)]


def pack_kernel(heads, groups, total, len_ref, do_ref, o_ref, q_ref, k_ref, v_ref, ex_ref, dk_ref, dv_ref, pay_ref, kv_ref, *refs):
    grad, out, query, keys, values, buf, packed, high, low, sems = refs
    rows = out.shape[0]
    wide = heads * D
    pairs = (
        (do_ref, grad), (o_ref, out), (q_ref, query), (k_ref, keys), (v_ref, values), (ex_ref, buf),
        (dk_ref, kv_ref.at[pl.ds(0, D)]), (dv_ref, kv_ref.at[pl.ds(D, D)]),
    )
    loads = [pltpu.make_async_copy(source, to, sems.at[n]) for n, (source, to) in enumerate(pairs)]
    for load in loads:
        load.start()
    sends = []

    def send(source, to, size):
        for g in range(groups):
            part = pay_ref.at[g, :, pl.ds(to, size)]
            sends.append(pltpu.make_async_copy(source.at[:, pl.ds(g * size, size)], part, sems.at[len(pairs) + len(sends)]))
            sends[-1].start()

    row = lax.axis_index("head") * rows + sublanes((rows, D))
    within = jnp.where(row < len_ref[0, 0], row, row - len_ref[0, 0])
    log_count = jnp.log((within + 1 + total).astype(F32))
    loads[0].wait()
    send(grad, wide, wide)
    loads[2].wait()
    send(query, 0, wide)
    loads[3].wait()
    send(keys, 2 * wide, D)
    loads[4].wait()
    send(values, 2 * wide + D, D)
    loads[1].wait()
    for g in range(groups):
        cut, at = slice(g * wide, (g + 1) * wide), slice(g * rows, (g + 1) * rows)
        high[at, :], low[at, :] = head_parts(out[:, cut], grad[:, cut])
    ones = head_ones((wide, D), 1)
    deltas = dot(high[...], ones, 1, 0) + dot(low[...], ones, 1, 0)
    loads[5].wait()
    lse = (buf[...] + log_count[:, : heads * groups]) * LOG2E
    lse = jnp.concatenate([lse, jnp.zeros((rows, D - heads * groups), F32)], axis=1)
    lane = lanes((rows, D))
    for g in range(groups):
        mine = lse if g == 0 else pltpu.roll(lse, D - heads * g, 1)
        mine = jnp.where(lane < heads, mine, 0.0)
        stats = jnp.zeros((rows, D), F32)
        for n, value in enumerate((mine, deltas[g * rows : (g + 1) * rows])):
            for m in range(3):
                part = value.astype(BF).astype(F32)
                value = value - part
                at = (3 * n + m) * 16
                stats = stats + (pltpu.roll(part, at, 1) if at else part)
        packed[g] = jnp.where(lane == 96, (row - within).astype(F32), stats).astype(BF)
    sends.append(pltpu.make_async_copy(packed, pay_ref.at[:, :, pl.ds(2 * wide + 2 * D, D)], sems.at[len(pairs) + len(sends)]))
    sends[-1].start()
    for copy in loads[6:] + sends:
        copy.wait()


def doc_keys(order_ref, me, ctx_size, piece):
    core, z = piece
    place, low, step = me // 4, (me // 2) % 2, ctx_size // 4
    depth = lax.rem(place + step - z, step)
    return [(depth * 2 + (low ^ x if isinstance(low, int) else lax.bitwise_xor(low, x))) * 2 + lax.bitwise_xor(lax.rem(me, 2), core) for x in range(2)]


def doc_lse(order_ref, me, owner, lse, lane_half):
    parts = []
    for b in range(2):
        kb = order_ref[2 * owner + b]
        bias = [jnp.where(kb <= order_ref[2 * me + a], 0.0, HIDDEN).astype(F32) for a in range(2)]
        parts.append(lse + jnp.where(lane_half, bias[1], bias[0]))
    return parts


def doc_kernel(core, heads, ctx_size, order_ref, *refs):
    kv_refs, refs = refs[:4], refs[4:]
    if core == 0:
        q_ref, o_ref, do_ref, ex_ref, *state, dq_ref, near_hbm, own_hbm, near_ref, own_ref, sems = refs
    else:
        *state, dq_in, far_hbm, dq_hbm, far_ref, dq_ref, sems = refs
    qs_ref, dos_ref, lse_ref, delta_ref = state
    stores = []

    def store(source, to):
        stores.append(pltpu.make_async_copy(source, to, sems.at[len(stores)]))
        stores[-1].start()

    me = lax.axis_index("ctx")
    rows = heads * D
    lane = lax.rem(lanes((1, rows)), D)
    half = D // 2
    lane_half = lane >= half
    if core == 0:
        one = lanes((1, D))
        pos = jnp.where(one < half, order_ref[2 * me] * half + one, order_ref[2 * me + 1] * half + one - half)
        spread_rows((ex_ref[...] + jnp.log((pos + 1).astype(F32))) * LOG2E, lse_ref, heads)
        stack_heads(q_ref, qs_ref, heads, 0)
        stack_heads(do_ref, dos_ref, heads, 0)
        ones = head_ones((16, rows), 0)
        high, low = head_parts(o_ref[...], do_ref[...])
        spread_rows(dot(ones, high, 1, 1) + dot(ones, low, 1, 1), delta_ref, heads)
    lse = lse_ref[...]
    delta = delta_ref[...]
    total = None
    for depth in range(4):
        owners = doc_keys(order_ref, me, ctx_size, (core, depth))
        shift = [row for o in owners for row in doc_lse(order_ref, me, o, lse, lane_half)]
        mask = None
        if core == 0 and depth == 0:
            key = sublanes((2 * D, 1))
            key_pos = jnp.where(key < half, order_ref[2 * me] * half + key, order_ref[2 * me + 1] * half + key - half)
            row_pos = jnp.where(lane_half, order_ref[2 * me + 1] * half + lane - half, order_ref[2 * me] * half + lane)
            mask = jnp.where(key < D, key_pos, -1) <= row_pos
        dq, dk, dv = pair_block(qs_ref, dos_ref, *both(kv_refs[depth]), shift, delta, mask)
        for side, grad in enumerate((dk, dv)):
            cut = slice(side * D, (side + 1) * D)
            if core == 0:
                own_ref[depth, :, cut] = grad[:D]
                near_ref[depth, :, cut] = grad[D:]
            else:
                far_ref[depth, :, cut] = grad
        total = dq if total is None else total + dq
        if core == 0:
            store(own_ref.at[depth], own_hbm.at[depth])
            store(near_ref.at[depth], near_hbm.at[depth])
        else:
            store(far_ref.at[depth], far_hbm.at[depth])
    if core == 0:
        dq_ref[...] = total
    else:
        dq_ref[...] = ((total + dq_in[...]) * SCALE).astype(BF)
        store(dq_ref, dq_hbm)
    for copy in stores:
        copy.wait()


def turn_kernel(heads, turned_ref, out_ref):
    for j in range(heads):
        out_ref[:, j * D : (j + 1) * D] = turned_ref[:, j * D : (j + 1) * D].T


def self_kernel(heads, pay_ref, qs_ref, dos_ref, lse_ref, delta_ref, self_ref, dq_ref):
    wide = heads * D
    stack_heads(pay_ref, qs_ref, heads, 0)
    stack_heads(pay_ref, dos_ref, heads, wide)
    stats = pay_ref[:, 2 * wide + 2 * D :].astype(F32).T
    spread_rows(stats[:16] + stats[16:32] + stats[32:48], lse_ref, heads)
    spread_rows(stats[48:64] + stats[64:80] + stats[80:96], delta_ref, heads)
    row = lanes((1, D))
    key = sublanes((D, 1))
    seen = (key <= row) & (key >= stats[96:97].astype(jnp.int32))
    mask = jnp.concatenate([seen] * heads, axis=1)
    keys = pay_ref[:, 2 * wide : 2 * wide + D]
    values = pay_ref[:, 2 * wide + D : 2 * wide + 2 * D]
    dq, dk, dv = pair_block(qs_ref, dos_ref, keys, values, lse_ref[...], delta_ref[...], mask)
    self_ref[:, :D] = dk.astype(BF)
    self_ref[:, D:] = dv.astype(BF)
    dq_ref[...] = dq


def far_kernel(qs_ref, dos_ref, lse_ref, delta_ref, dq_in, *refs):
    kv_refs, doc_ref = refs[:4], refs[4]
    send_ref, dq_ref = refs[5:]
    lse, delta = lse_ref[...], delta_ref[...]
    total = dq_in[...]
    for n in range(4):
        dq, dk, dv = pair_block(qs_ref, dos_ref, *both(kv_refs[n]), lse, delta, None)
        send_ref[n, :, :D] = (dk + doc_ref[n, :, :D]).astype(BF)
        send_ref[n, :, D:] = (dv + doc_ref[n, :, D:]).astype(BF)
        total = total + dq
    dq_ref[...] = total


def column(x, qs_ref, dos_ref, lse, delta, kv_refs, total, store):
    for pair in range(len(kv_refs) // 2):
        refs = [kv_refs[2 * pair + m] for m in range(2)]
        keys = jnp.concatenate([ref[2 * x * D : 2 * x * D + D] for ref in refs], axis=0)
        values = jnp.concatenate([ref[2 * x * D + D : 2 * x * D + 2 * D] for ref in refs], axis=0)
        dq, dk, dv = pair_block(qs_ref, dos_ref, keys, values, lse, delta, None)
        for m in range(2):
            part = slice(m * D, (m + 1) * D)
            store(2 * pair + m, slice(0, D), dk[part])
            store(2 * pair + m, slice(D, 2 * D), dv[part])
        total = total + dq
    return total


def near_kernel(qs_ref, dos_ref, lse_ref, delta_ref, dq_in, core_ref, *refs):
    kv_refs, doc_ref = refs[:4], refs[4]
    send_ref, dq_ref = refs[5:]

    def store(n, cut, grad):
        send_ref[n, :, cut] = (grad + doc_ref[n, :, cut] + core_ref[n, D:, cut].astype(F32)).astype(BF)

    dq_ref[...] = column(1, qs_ref, dos_ref, lse_ref[...], delta_ref[...], kv_refs, dq_in[...], store)


def own_kernel(qs_ref, dos_ref, lse_ref, delta_ref, dq_in, *refs):
    kv_refs = refs[:2]
    out_ref, dq_ref = refs[2:]

    def store(n, cut, grad):
        out_ref[n, :, cut] = grad

    dq_ref[...] = column(0, qs_ref, dos_ref, lse_ref[...], delta_ref[...], kv_refs, dq_in[...], store)


def last_kernel(heads, groups, qs_ref, dos_ref, lse_ref, delta_ref, dq_in, self_ref, *refs):
    kv_refs = refs[:2]
    out_ref, back_ref = refs[2:]
    wide = heads * D

    def store(n, cut, grad):
        out_ref[n, :, cut] = grad

    total = column(0, qs_ref, dos_ref, lse_ref[...], delta_ref[...], kv_refs, dq_in[...], store)
    each = D // groups
    for g in range(groups):
        back_ref[g, :, wide:] = self_ref[g * each : (g + 1) * each]
    for j, part in enumerate(unstack_query_grad(total, heads)):
        for g in range(groups):
            back_ref[g, :, j * D : (j + 1) * D] = part[g * each : (g + 1) * each]


def held_kernel(low_ref, high_ref, doc_ref, core_ref, chip_ref, keep_ref, *send_refs):
    for n in range(4):
        own = low_ref[n] if n < 2 else high_ref[n - 2]
        held = own + doc_ref[n] + core_ref[n, :D].astype(F32) + chip_ref[n].astype(F32)
        if n == 0:
            keep_ref[...] = held
        else:
            send_refs[n - 1][...] = held.astype(BF)


def unpack_kernel(heads, groups, back_ref, keep_ref, *refs):
    q_ref, k_ref, v_ref, dk_ref, dv_ref = refs[3:]
    wide = heads * D
    total = keep_ref[...]
    for ref in refs[:3]:
        total = total + ref[...].astype(F32)
    dk_ref[...] = total[:, :D].astype(BF)
    dv_ref[...] = total[:, D:].astype(BF)
    for g in range(groups):
        q_ref[:, g * wide : (g + 1) * wide] = back_ref[g, :, :wide]
        k_ref[:, g * D : (g + 1) * D] = back_ref[g, :, wide : wide + D]
        v_ref[:, g * D : (g + 1) * D] = back_ref[g, :, wide + D :]


def local(
    block_order,
    question_lengths,
    document_query_matrix,
    document_key_matrix,
    document_value_matrix,
    document_output,
    document_outgrad,
    document_excess,
    question_query_matrix,
    question_key_matrix,
    question_value_matrix,
    question_output,
    question_outgrad,
    question_excess,
):
    ctx_size, groups = lax.axis_size("ctx"), lax.axis_size("head")
    heads = document_excess.shape[1]
    rows, each = document_query_matrix.shape[0], question_query_matrix.shape[0]
    total_doc = rows * ctx_size
    wide, stacked = heads * D, heads * rows
    depth = ctx_size // 4

    def other_core(x):
        return lax.ppermute(x, "ctx", [(i, i ^ 1) for i in range(ctx_size)])

    def other_chip(x):
        return lax.ppermute(x, "ctx", [(i, i ^ 2) for i in range(ctx_size)])

    def along_z(x, d):
        return lax.ppermute(x, "ctx", [(i, (i + 4 * d) % ctx_size) for i in range(ctx_size)])

    chip = [other_chip(document_key_matrix), other_chip(document_value_matrix)]
    asking = pltpu.VMEM((each, wide * groups), BF)
    narrow = pltpu.VMEM((each, D * groups), BF)
    both_parts = pltpu.VMEM((groups * each, wide), BF)
    payload, kv = pl.pallas_call(
        functools.partial(pack_kernel, heads, groups, total_doc),
        out_shape=(
            pltpu.HBM((groups, each, 2 * wide + 3 * D), BF),
            jax.ShapeDtypeStruct((4 * rows, D), BF),
        ),
        in_specs=[smem()] + [hbm()] * 8,
        out_specs=(hbm(), vmem()),
        scratch_shapes=[asking, asking, asking, narrow, narrow, pltpu.VMEM((each, heads * groups), F32)]
        + [pltpu.VMEM((groups, each, D), BF), both_parts, both_parts, pltpu.SemaphoreType.DMA((9 + 4 * groups,))],
        compiler_params=SHARED,
        cost_estimate=cost(5),
    )(
        question_lengths,
        *[
            pltpu.with_memory_space_constraint(x, pltpu.HBM)
            for x in (
                question_outgrad, question_output, question_query_matrix, question_key_matrix, question_value_matrix,
                question_excess, document_key_matrix, document_value_matrix,
            )
        ],
    )
    here = kv
    for n, part in enumerate(chip):
        here = lax.dynamic_update_slice(here, part, ((2 + n) * rows, 0))
    mine = [here] + [along_z(here, d) for d in range(1, depth)]
    theirs = [other_core(piece) for piece in mine]
    asked = lax.all_to_all(payload, "head", 0, 0, tiled=True).reshape(groups * each, -1)

    quarter = ((depth, rows, 2 * D), F32)
    double = ((depth, 2 * rows, 2 * D), F32)
    row_state = [((stacked, D), BF), ((stacked, D), BF), ((1, stacked), F32), ((1, stacked), F32)]
    query_sum = ((D, stacked), F32)
    flat = ((rows, wide), BF)

    def document(core, outs, partial, *args):
        return pl.pallas_call(
            functools.partial(doc_kernel, core, heads, ctx_size),
            out_shape=tuple(jax.ShapeDtypeStruct(*out) for out in outs) + tuple(pltpu.HBM(*out) for out in partial),
            in_specs=[smem()] + [vmem()] * (len(args) - 1),
            out_specs=(vmem(),) * len(outs) + (hbm(),) * len(partial),
            scratch_shapes=[pltpu.VMEM(*out) for out in partial] + [pltpu.SemaphoreType.DMA((8,))],
            compiler_params=SHARED,
            cost_estimate=cost(6),
        )(*args)

    *doc_state, dq, near_doc, own_doc = document(
        0,
        row_state + [query_sum],
        [quarter, quarter],
        block_order, *mine, document_query_matrix, document_output, document_outgrad, document_excess.T,
    )
    far_doc, doc_turned = document(1, [], [double, ((D, stacked), BF)], block_order, *theirs, *doc_state, dq)
    *state, own_self, dq = call(
        1.5,
        functools.partial(self_kernel, heads),
        row_state + [((rows, 2 * D), BF), query_sum],
        0,
        asked,
    )
    far, dq = call(4.4, far_kernel, [((depth, 2 * rows, 2 * D), BF), query_sum], 0, *state, dq, *theirs, far_doc)
    core_sum = other_core(far)
    low, dq = call(1.5, own_kernel, [((2, rows, 2 * D), F32), query_sum], 0, *state, dq, *mine[:2])
    near, dq = call(2.2, near_kernel, [((depth, rows, 2 * D), BF), query_sum], 0, *state, dq, core_sum, *mine, near_doc)
    chip_sum = other_chip(near)
    high, back = call(
        2,
        functools.partial(last_kernel, heads, groups),
        [((2, rows, 2 * D), F32), ((groups, each, wide + 2 * D), BF)],
        0,
        *state, dq, own_self, *mine[2:],
    )
    back = lax.all_to_all(back, "head", 0, 0, tiled=True)
    keep, *sends = call(
        25,
        held_kernel,
        [((rows, 2 * D), F32)] + [((rows, 2 * D), BF)] * (depth - 1),
        0,
        low, high, own_doc, core_sum, chip_sum,
    )
    (document_query_grad,) = call(2, functools.partial(turn_kernel, heads), [flat], 0, doc_turned)
    arrived = [along_z(send, depth - 1 - n) for n, send in enumerate(sends)]
    question_query_grad, question_keys_grad, question_values_grad, document_keys_grad, document_values_grad = call(
        0.8,
        functools.partial(unpack_kernel, heads, groups),
        [((each, wide * groups), BF), ((each, D * groups), BF), ((each, D * groups), BF), ((rows, D), BF), ((rows, D), BF)],
        0,
        back, keep, *arrived,
    )
    return (
        document_query_grad,
        document_keys_grad,
        document_values_grad,
        question_query_grad,
        question_keys_grad,
        question_values_grad,
    )


def solution(mesh):
    return jax.shard_map(
        local,
        mesh=mesh,
        in_specs=(
            P(),
            P("ctx", None),
            P("ctx", "head"),
            P("ctx", "head"),
            P("ctx", "head"),
            P("ctx", "head"),
            P("ctx", "head"),
            P("ctx", "head"),
            P(("ctx", "head"), None),
            P(("ctx", "head"), None),
            P(("ctx", "head"), None),
            P(("ctx", "head"), None),
            P(("ctx", "head"), None),
            P(("ctx", "head"), None),
        ),
        out_specs=(
            P("ctx", "head"),
            P("ctx", "head"),
            P("ctx", "head"),
            P(("ctx", "head"), None),
            P(("ctx", "head"), None),
            P(("ctx", "head"), None),
        ),
        check_vma=False,
    )
```

```python
import functools

import jax
import jax.numpy as jnp
from jax import lax
from jax.experimental import pallas as pl
from jax.experimental.pallas import tpu as pltpu
from jax.sharding import PartitionSpec as P

D = 128
SCALE = D**-0.5
LOG2E = 1.4426950408889634
HIDDEN = 1e30
BF = jnp.bfloat16
F32 = jnp.float32
SHARED = pltpu.CompilerParams(vmem_limit_bytes=20 * 2**20)
WHOLE = pltpu.CompilerParams(vmem_limit_bytes=60 * 2**20)


def dot(a, b, ca, cb):
    return lax.dot_general(a, b, (((ca,), (cb,)), ((), ())), preferred_element_type=F32)


def lanes(shape):
    return lax.broadcasted_iota(jnp.int32, shape, 1)


def sublanes(shape):
    return lax.broadcasted_iota(jnp.int32, shape, 0)


def smem():
    return pl.BlockSpec(memory_space=pltpu.SMEM)


def vmem():
    return pl.BlockSpec(memory_space=pltpu.VMEM)


def hbm():
    return pl.BlockSpec(memory_space=pltpu.HBM)


def cost(us):
    return pl.CostEstimate(flops=int(us * 1.1e9), bytes_accessed=0, transcendentals=0)


def call(us, body, outs, n_smem, *args, **kw):
    return pl.pallas_call(
        body,
        out_shape=tuple(jax.ShapeDtypeStruct(s, t) for s, t in outs),
        in_specs=[smem()] * n_smem + [vmem()] * (len(args) - n_smem),
        out_specs=tuple(vmem() for _ in outs),
        compiler_params=SHARED,
        cost_estimate=cost(us),
        **kw,
    )(*args)


def pair_block(qs_ref, dos_ref, keys, values, lse, delta, mask):
    scores = dot(keys, qs_ref[...], 1, 1)
    dprob = dot(values, dos_ref[...], 1, 1)
    scores = scores * (SCALE * LOG2E)
    if isinstance(lse, list):
        step = scores.shape[0] // len(lse)
        prob = jnp.concatenate([jnp.exp2(scores[n * step : (n + 1) * step] - row) for n, row in enumerate(lse)], axis=0)
    else:
        prob = jnp.exp2(scores - lse)
    if mask is not None:
        prob = jnp.where(mask, prob, 0.0)
    dscore = (prob * (dprob - delta)).astype(BF)
    dv = dot(prob.astype(BF), dos_ref[...], 1, 0)
    dk = dot(dscore, qs_ref[...], 1, 0) * SCALE
    dq = dot(keys, dscore, 0, 0)
    return dq, dk, dv


def both(ref):
    keys = jnp.concatenate([ref[:D], ref[2 * D : 3 * D]], axis=0)
    values = jnp.concatenate([ref[D : 2 * D], ref[3 * D :]], axis=0)
    return keys, values


def head_parts(out, grad):
    product = out.astype(F32) * grad.astype(F32)
    high = product.astype(BF)
    return high, (product - high.astype(F32)).astype(BF)


def head_ones(shape, axis):
    position = lax.broadcasted_iota(jnp.int32, shape, 1 - axis) // D
    return jnp.where(position == lax.broadcasted_iota(jnp.int32, shape, axis), 1.0, 0.0).astype(BF)


def stack_heads(source, target, heads, first):
    for j in range(heads):
        at = first + j * D
        target[j * D : (j + 1) * D, :] = source[:, at : at + D]


def spread_rows(rows, target, heads):
    for j in range(heads):
        target[:, j * D : (j + 1) * D] = rows[j : j + 1, :]


def unstack_query_grad(dq, heads):
    dq = (dq * SCALE).astype(BF)
    return [dq[:, j * D : (j + 1) * D].T for j in range(heads)]


def pack_kernel(heads, groups, total, len_hbm, do_ref, o_ref, q_ref, k_ref, v_ref, ex_ref, dk_ref, dv_ref, pay_ref, kv_ref, *refs):
    grad, out, query, keys, values, buf, len_ref, packed, high, low, sems = refs
    rows = out.shape[0]
    wide = heads * D
    pairs = (
        (do_ref, grad), (o_ref, out), (q_ref, query), (k_ref, keys), (v_ref, values), (ex_ref, buf), (len_hbm, len_ref),
        (dk_ref, kv_ref.at[pl.ds(0, D)]), (dv_ref, kv_ref.at[pl.ds(D, D)]),
    )
    loads = [pltpu.make_async_copy(source, to, sems.at[n]) for n, (source, to) in enumerate(pairs)]
    for load in loads:
        load.start()
    sends = []

    def send(source, to, size):
        for g in range(groups):
            part = pay_ref.at[g, :, pl.ds(to, size)]
            sends.append(pltpu.make_async_copy(source.at[:, pl.ds(g * size, size)], part, sems.at[len(pairs) + len(sends)]))
            sends[-1].start()

    loads[0].wait()
    send(grad, wide, wide)
    loads[2].wait()
    send(query, 0, wide)
    loads[3].wait()
    send(keys, 2 * wide, D)
    loads[4].wait()
    send(values, 2 * wide + D, D)
    loads[1].wait()
    for g in range(groups):
        cut, at = slice(g * wide, (g + 1) * wide), slice(g * rows, (g + 1) * rows)
        high[at, :], low[at, :] = head_parts(out[:, cut], grad[:, cut])
    ones = head_ones((wide, D), 1)
    deltas = dot(high[...], ones, 1, 0) + dot(low[...], ones, 1, 0)
    loads[5].wait()
    loads[6].wait()
    row = lax.axis_index("head") * rows + sublanes((rows, D))
    within = jnp.where(row < len_ref[0, 0], row, row - len_ref[0, 0])
    log_count = jnp.log((within + 1 + total).astype(F32))
    lse = (buf[...] + log_count[:, : heads * groups]) * LOG2E
    lse = jnp.concatenate([lse, jnp.zeros((rows, D - heads * groups), F32)], axis=1)
    lane = lanes((rows, D))
    for g in range(groups):
        mine = lse if g == 0 else pltpu.roll(lse, D - heads * g, 1)
        mine = jnp.where(lane < heads, mine, 0.0)
        stats = jnp.zeros((rows, D), F32)
        for n, value in enumerate((mine, deltas[g * rows : (g + 1) * rows])):
            for m in range(3):
                part = value.astype(BF).astype(F32)
                value = value - part
                at = (3 * n + m) * 16
                stats = stats + (pltpu.roll(part, at, 1) if at else part)
        packed[g] = jnp.where(lane == 96, (row - within).astype(F32), stats).astype(BF)
    sends.append(pltpu.make_async_copy(packed, pay_ref.at[:, :, pl.ds(2 * wide + 2 * D, D)], sems.at[len(pairs) + len(sends)]))
    sends[-1].start()
    for copy in loads[7:] + sends:
        copy.wait()


def doc_keys(order_ref, me, ctx_size, piece):
    core, z = piece
    place, low, step = me // 4, (me // 2) % 2, ctx_size // 4
    depth = lax.rem(place + step - z, step)
    return [(depth * 2 + (low ^ x if isinstance(low, int) else lax.bitwise_xor(low, x))) * 2 + lax.bitwise_xor(lax.rem(me, 2), core) for x in range(2)]


def doc_lse(order_ref, me, owner, lse, lane_half):
    parts = []
    for b in range(2):
        kb = order_ref[2 * owner + b]
        bias = [jnp.where(kb <= order_ref[2 * me + a], 0.0, HIDDEN).astype(F32) for a in range(2)]
        parts.append(lse + jnp.where(lane_half, bias[1], bias[0]))
    return parts


def doc_kernel(core, heads, ctx_size, order_ref, *refs):
    kv_refs, refs = refs[:4], refs[4:]
    if core == 0:
        q_ref, o_ref, do_ref, ex_ref, *state, dq_ref, near_hbm, own_hbm, near_ref, own_ref, sems = refs
    else:
        *state, dq_in, far_hbm, dq_hbm, far_ref, dq_ref, sems = refs
    qs_ref, dos_ref, lse_ref, delta_ref = state
    stores = []

    def store(source, to):
        stores.append(pltpu.make_async_copy(source, to, sems.at[len(stores)]))
        stores[-1].start()

    me = lax.axis_index("ctx")
    rows = heads * D
    lane = lax.rem(lanes((1, rows)), D)
    half = D // 2
    lane_half = lane >= half
    if core == 0:
        one = lanes((1, D))
        pos = jnp.where(one < half, order_ref[2 * me] * half + one, order_ref[2 * me + 1] * half + one - half)
        spread_rows((ex_ref[...] + jnp.log((pos + 1).astype(F32))) * LOG2E, lse_ref, heads)
        stack_heads(q_ref, qs_ref, heads, 0)
        stack_heads(do_ref, dos_ref, heads, 0)
        ones = head_ones((16, rows), 0)
        high, low = head_parts(o_ref[...], do_ref[...])
        spread_rows(dot(ones, high, 1, 1) + dot(ones, low, 1, 1), delta_ref, heads)
    lse = lse_ref[...]
    delta = delta_ref[...]
    total = None
    for depth in range(4):
        owners = doc_keys(order_ref, me, ctx_size, (core, depth))
        shift = [row for o in owners for row in doc_lse(order_ref, me, o, lse, lane_half)]
        mask = None
        if core == 0 and depth == 0:
            key = sublanes((2 * D, 1))
            key_pos = jnp.where(key < half, order_ref[2 * me] * half + key, order_ref[2 * me + 1] * half + key - half)
            row_pos = jnp.where(lane_half, order_ref[2 * me + 1] * half + lane - half, order_ref[2 * me] * half + lane)
            mask = jnp.where(key < D, key_pos, -1) <= row_pos
        dq, dk, dv = pair_block(qs_ref, dos_ref, *both(kv_refs[depth]), shift, delta, mask)
        for side, grad in enumerate((dk, dv)):
            cut = slice(side * D, (side + 1) * D)
            if core == 0:
                own_ref[depth, :, cut] = grad[:D]
                near_ref[depth, :, cut] = grad[D:]
            else:
                far_ref[depth, :, cut] = grad
        total = dq if total is None else total + dq
        if depth % 2 == 1:
            done = pl.ds(depth - 1, 2)
            if core == 0:
                store(own_ref.at[done], own_hbm.at[done])
                store(near_ref.at[done], near_hbm.at[done])
            else:
                store(far_ref.at[done], far_hbm.at[done])
    if core == 0:
        dq_ref[...] = total
    else:
        dq_ref[...] = ((total + dq_in[...]) * SCALE).astype(BF)
        store(dq_ref, dq_hbm)
    for copy in stores:
        copy.wait()


def turn_kernel(heads, turned_ref, out_ref):
    for j in range(heads):
        out_ref[:, j * D : (j + 1) * D] = turned_ref[:, j * D : (j + 1) * D].T


def far_kernel(heads, pay_ref, *refs):
    kv_refs, doc_hbm = refs[:4], refs[4]
    send_ref, dq_ref, qs_ref, dos_ref, lse_ref, delta_ref, doc_ref, sems = refs[5:]
    parts = (pl.ds(0, 1), pl.ds(1, 3))
    loads = [pltpu.make_async_copy(doc_hbm.at[at], doc_ref.at[at], sems.at[n]) for n, at in enumerate(parts)]
    for load in loads:
        load.start()
    wide = heads * D
    stack_heads(pay_ref, qs_ref, heads, 0)
    stack_heads(pay_ref, dos_ref, heads, wide)
    stats = pay_ref[:, 2 * wide + 2 * D :].astype(F32).T
    spread_rows(stats[:16] + stats[16:32] + stats[32:48], lse_ref, heads)
    spread_rows(stats[48:64] + stats[64:80] + stats[80:96], delta_ref, heads)
    lse, delta = lse_ref[...], delta_ref[...]
    total = None
    for n in range(4):
        dq, dk, dv = pair_block(qs_ref, dos_ref, *both(kv_refs[n]), lse, delta, None)
        if n < 2:
            loads[n].wait()
        send_ref[n, :, :D] = (dk + doc_ref[n, :, :D]).astype(BF)
        send_ref[n, :, D:] = (dv + doc_ref[n, :, D:]).astype(BF)
        total = dq if total is None else total + dq
    dq_ref[...] = total


def column(x, qs_ref, dos_ref, lse, delta, kv_refs, total, store):
    for pair in range(len(kv_refs) // 2):
        refs = [kv_refs[2 * pair + m] for m in range(2)]
        keys = jnp.concatenate([ref[2 * x * D : 2 * x * D + D] for ref in refs], axis=0)
        values = jnp.concatenate([ref[2 * x * D + D : 2 * x * D + 2 * D] for ref in refs], axis=0)
        dq, dk, dv = pair_block(qs_ref, dos_ref, keys, values, lse, delta, None)
        for m in range(2):
            part = slice(m * D, (m + 1) * D)
            store(2 * pair + m, slice(0, D), dk[part])
            store(2 * pair + m, slice(D, 2 * D), dv[part])
        total = total + dq
    return total


def near_kernel(qs_ref, dos_ref, lse_ref, delta_ref, dq_in, core_ref, *refs):
    kv_refs, doc_ref = refs[:4], refs[4]
    send_ref, dq_ref = refs[5:]

    def store(n, cut, grad):
        send_ref[n, :, cut] = (grad + doc_ref[n, :, cut] + core_ref[n, D:, cut].astype(F32)).astype(BF)

    dq_ref[...] = column(1, qs_ref, dos_ref, lse_ref[...], delta_ref[...], kv_refs, dq_in[...], store)


def own_kernel(heads, qs_ref, dos_ref, lse_ref, delta_ref, dq_in, pay_ref, *refs):
    kv_refs = refs[:2]
    out_ref, self_ref, dq_ref = refs[2:]
    wide = heads * D
    lse, delta = lse_ref[...], delta_ref[...]
    stats = pay_ref[:, 2 * wide + 2 * D :].astype(F32).T
    row = lanes((1, D))
    key = sublanes((D, 1))
    seen = (key <= row) & (key >= stats[96:97].astype(jnp.int32))
    mask = jnp.concatenate([seen] * heads, axis=1)
    keys = pay_ref[:, 2 * wide : 2 * wide + D]
    values = pay_ref[:, 2 * wide + D : 2 * wide + 2 * D]
    dq, dk, dv = pair_block(qs_ref, dos_ref, keys, values, lse, delta, mask)
    self_ref[:, :D] = dk.astype(BF)
    self_ref[:, D:] = dv.astype(BF)

    def store(n, cut, grad):
        out_ref[n, :, cut] = grad

    dq_ref[...] = column(0, qs_ref, dos_ref, lse, delta, kv_refs, dq_in[...] + dq, store)


def last_kernel(heads, groups, qs_ref, dos_ref, lse_ref, delta_ref, dq_in, self_ref, low_ref, core_ref, doc_ref, *refs):
    kv_refs = refs[:2]
    out_ref, back_hbm, back_ref, sems = refs[2:]
    wide = heads * D
    each = D // groups
    copies = []

    def send(at, size):
        cut = (slice(None), slice(None), pl.ds(at, size))
        copies.append(pltpu.make_async_copy(back_ref.at[cut], back_hbm.at[cut], sems.at[len(copies)]))
        copies[-1].start()

    for g in range(groups):
        back_ref[g, :, wide:] = self_ref[g * each : (g + 1) * each]
    send(wide, 2 * D)

    def other(n, cut):
        return doc_ref[n, :, cut] + core_ref[n, :D, cut].astype(F32)

    def store(n, cut, grad):
        out_ref[n + 2, :, cut] = grad + other(n + 2, cut)

    total = column(0, qs_ref, dos_ref, lse_ref[...], delta_ref[...], kv_refs, dq_in[...], store)
    for j, part in enumerate(unstack_query_grad(total, heads)):
        for g in range(groups):
            back_ref[g, :, j * D : (j + 1) * D] = part[g * each : (g + 1) * each]
        if j % 4 == 3:
            send((j - 3) * D, 4 * D)
    for n in range(2):
        out_ref[n] = low_ref[n] + other(n, slice(0, 2 * D))
    for copy in copies:
        copy.wait()


def held_kernel(own_ref, chip_ref, keep_ref, *send_refs):
    for n in range(4):
        held = own_ref[n] + chip_ref[n].astype(F32)
        if n == 0:
            keep_ref[...] = held
        else:
            send_refs[n - 1][...] = held.astype(BF)


def unpack_kernel(heads, groups, back_ref, keep_ref, *refs):
    q_ref, k_ref, v_ref, dk_ref, dv_ref = refs[3:]
    wide = heads * D
    total = keep_ref[...]
    for ref in refs[:3]:
        total = total + ref[...].astype(F32)
    dk_ref[...] = total[:, :D].astype(BF)
    dv_ref[...] = total[:, D:].astype(BF)
    for g in range(groups):
        q_ref[:, g * wide : (g + 1) * wide] = back_ref[g, :, :wide]
        k_ref[:, g * D : (g + 1) * D] = back_ref[g, :, wide : wide + D]
        v_ref[:, g * D : (g + 1) * D] = back_ref[g, :, wide + D :]


def local(
    block_order,
    question_lengths,
    document_query_matrix,
    document_key_matrix,
    document_value_matrix,
    document_output,
    document_outgrad,
    document_excess,
    question_query_matrix,
    question_key_matrix,
    question_value_matrix,
    question_output,
    question_outgrad,
    question_excess,
):
    ctx_size, groups = lax.axis_size("ctx"), lax.axis_size("head")
    heads = document_excess.shape[1]
    rows, each = document_query_matrix.shape[0], question_query_matrix.shape[0]
    total_doc = rows * ctx_size
    wide, stacked = heads * D, heads * rows
    depth = ctx_size // 4

    def other_core(x):
        return lax.ppermute(x, "ctx", [(i, i ^ 1) for i in range(ctx_size)])

    def other_chip(x):
        return lax.ppermute(x, "ctx", [(i, i ^ 2) for i in range(ctx_size)])

    def along_z(x, d):
        return lax.ppermute(x, "ctx", [(i, (i + 4 * d) % ctx_size) for i in range(ctx_size)])

    chip = [other_chip(document_key_matrix), other_chip(document_value_matrix)]
    asking = pltpu.VMEM((each, wide * groups), BF)
    narrow = pltpu.VMEM((each, D * groups), BF)
    both_parts = pltpu.VMEM((groups * each, wide), BF)
    payload, kv = pl.pallas_call(
        functools.partial(pack_kernel, heads, groups, total_doc),
        out_shape=(
            pltpu.HBM((groups, each, 2 * wide + 3 * D), BF),
            jax.ShapeDtypeStruct((4 * rows, D), BF),
        ),
        in_specs=[hbm()] * 9,
        out_specs=(hbm(), vmem()),
        scratch_shapes=[asking, asking, asking, narrow, narrow, pltpu.VMEM((each, heads * groups), F32)]
        + [pltpu.SMEM(question_lengths.shape, jnp.int32), pltpu.VMEM((groups, each, D), BF), both_parts, both_parts]
        + [pltpu.SemaphoreType.DMA((10 + 4 * groups,))],
        compiler_params=SHARED,
        cost_estimate=cost(5),
    )(
        *[
            pltpu.with_memory_space_constraint(x, pltpu.HBM)
            for x in (
                question_lengths, question_outgrad, question_output, question_query_matrix, question_key_matrix,
                question_value_matrix, question_excess, document_key_matrix, document_value_matrix,
            )
        ],
    )
    here = kv
    for n, part in enumerate(chip):
        here = lax.dynamic_update_slice(here, part, ((2 + n) * rows, 0))
    mine = [here] + [along_z(here, d) for d in range(1, depth)]
    theirs = [other_core(piece) for piece in mine]
    asked = lax.all_to_all(payload, "head", 0, 0, tiled=True).reshape(groups * each, -1)

    quarter = ((depth, rows, 2 * D), F32)
    double = ((depth, 2 * rows, 2 * D), F32)
    row_state = [((stacked, D), BF), ((stacked, D), BF), ((1, stacked), F32), ((1, stacked), F32)]
    query_sum = ((D, stacked), F32)
    flat = ((rows, wide), BF)

    def document(core, outs, partial, *args):
        return pl.pallas_call(
            functools.partial(doc_kernel, core, heads, ctx_size),
            out_shape=tuple(jax.ShapeDtypeStruct(*out) for out in outs) + tuple(pltpu.HBM(*out) for out in partial),
            in_specs=[smem()] + [vmem()] * (len(args) - 1),
            out_specs=(vmem(),) * len(outs) + (hbm(),) * len(partial),
            scratch_shapes=[pltpu.VMEM(*out) for out in partial] + [pltpu.SemaphoreType.DMA((8,))],
            compiler_params=SHARED,
            cost_estimate=cost(6),
        )(*args)

    *doc_state, dq, near_doc, own_doc = document(
        0,
        row_state + [query_sum],
        [quarter, quarter],
        block_order, *mine, document_query_matrix, document_output, document_outgrad, document_excess.T,
    )
    far_doc, doc_turned = document(1, [], [double, ((D, stacked), BF)], block_order, *theirs, *doc_state, dq)
    far, dq, *state = pl.pallas_call(
        functools.partial(far_kernel, heads),
        out_shape=tuple(jax.ShapeDtypeStruct(*out) for out in [((depth, 2 * rows, 2 * D), BF), query_sum] + row_state),
        in_specs=[vmem()] * 5 + [hbm()],
        out_specs=(vmem(),) * 6,
        scratch_shapes=[pltpu.VMEM(*double), pltpu.SemaphoreType.DMA((2,))],
        compiler_params=SHARED,
        cost_estimate=cost(4.8),
    )(asked, *theirs, pltpu.with_memory_space_constraint(far_doc, pltpu.HBM))
    core_sum = other_core(far)
    low, own_self, dq = call(
        2,
        functools.partial(own_kernel, heads),
        [((2, rows, 2 * D), F32), ((rows, 2 * D), BF), query_sum],
        0,
        *state, dq, asked, *mine[:2],
    )
    near, dq = call(2.2, near_kernel, [((depth, rows, 2 * D), BF), query_sum], 0, *state, dq, core_sum, *mine, near_doc)
    chip_sum = other_chip(near)
    returned = ((groups, each, wide + 2 * D), BF)
    own, back = pl.pallas_call(
        functools.partial(last_kernel, heads, groups),
        out_shape=(jax.ShapeDtypeStruct(*quarter), pltpu.HBM(*returned)),
        in_specs=[vmem()] * 11,
        out_specs=(vmem(), hbm()),
        scratch_shapes=[pltpu.VMEM(*returned), pltpu.SemaphoreType.DMA((4,))],
        compiler_params=SHARED,
        cost_estimate=cost(2),
    )(*state, dq, own_self, low, core_sum, own_doc, *mine[2:])
    back = lax.all_to_all(back, "head", 0, 0, tiled=True)
    keep, *sends = call(
        25,
        held_kernel,
        [((rows, 2 * D), F32)] + [((rows, 2 * D), BF)] * (depth - 1),
        0,
        own, chip_sum,
    )
    (document_query_grad,) = call(2, functools.partial(turn_kernel, heads), [flat], 0, doc_turned)
    arrived = [along_z(send, depth - 1 - n) for n, send in enumerate(sends)]
    question_query_grad, question_keys_grad, question_values_grad, document_keys_grad, document_values_grad = call(
        0.8,
        functools.partial(unpack_kernel, heads, groups),
        [((each, wide * groups), BF), ((each, D * groups), BF), ((each, D * groups), BF), ((rows, D), BF), ((rows, D), BF)],
        0,
        back, keep, *arrived,
    )
    return (
        document_query_grad,
        document_keys_grad,
        document_values_grad,
        question_query_grad,
        question_keys_grad,
        question_values_grad,
    )


def solution(mesh):
    return jax.shard_map(
        local,
        mesh=mesh,
        in_specs=(
            P(),
            P("ctx", None),
            P("ctx", "head"),
            P("ctx", "head"),
            P("ctx", "head"),
            P("ctx", "head"),
            P("ctx", "head"),
            P("ctx", "head"),
            P(("ctx", "head"), None),
            P(("ctx", "head"), None),
            P(("ctx", "head"), None),
            P(("ctx", "head"), None),
            P(("ctx", "head"), None),
            P(("ctx", "head"), None),
        ),
        out_specs=(
            P("ctx", "head"),
            P("ctx", "head"),
            P("ctx", "head"),
            P(("ctx", "head"), None),
            P(("ctx", "head"), None),
            P(("ctx", "head"), None),
        ),
        check_vma=False,
    )
```

```python
import functools

import jax
import jax.numpy as jnp
from jax import lax
from jax.experimental import pallas as pl
from jax.experimental.pallas import tpu as pltpu
from jax.sharding import PartitionSpec as P

D = 128
SCALE = D**-0.5
LOG2E = 1.4426950408889634
HIDDEN = 1e30
BF = jnp.bfloat16
F32 = jnp.float32
SHARED = pltpu.CompilerParams(vmem_limit_bytes=20 * 2**20)
WHOLE = pltpu.CompilerParams(vmem_limit_bytes=60 * 2**20)


def dot(a, b, ca, cb):
    return lax.dot_general(a, b, (((ca,), (cb,)), ((), ())), preferred_element_type=F32)


def lanes(shape):
    return lax.broadcasted_iota(jnp.int32, shape, 1)


def sublanes(shape):
    return lax.broadcasted_iota(jnp.int32, shape, 0)


def smem():
    return pl.BlockSpec(memory_space=pltpu.SMEM)


def vmem():
    return pl.BlockSpec(memory_space=pltpu.VMEM)


def hbm():
    return pl.BlockSpec(memory_space=pltpu.HBM)


def cost(us):
    return pl.CostEstimate(flops=int(us * 1.1e9), bytes_accessed=0, transcendentals=0)


def call(us, body, outs, n_smem, *args, **kw):
    return pl.pallas_call(
        body,
        out_shape=tuple(jax.ShapeDtypeStruct(s, t) for s, t in outs),
        in_specs=[smem()] * n_smem + [vmem()] * (len(args) - n_smem),
        out_specs=tuple(vmem() for _ in outs),
        compiler_params=SHARED,
        cost_estimate=cost(us),
        **kw,
    )(*args)


def pair_block(qs_ref, dos_ref, keys, values, lse, delta, mask):
    scores = dot(keys, qs_ref[...], 1, 1)
    dprob = dot(values, dos_ref[...], 1, 1)
    scores = scores * (SCALE * LOG2E)
    if isinstance(lse, list):
        step = scores.shape[0] // len(lse)
        prob = jnp.concatenate([jnp.exp2(scores[n * step : (n + 1) * step] - row) for n, row in enumerate(lse)], axis=0)
    else:
        prob = jnp.exp2(scores - lse)
    if mask is not None:
        prob = jnp.where(mask, prob, 0.0)
    dscore = (prob * (dprob - delta)).astype(BF)
    dv = dot(prob.astype(BF), dos_ref[...], 1, 0)
    dk = dot(dscore, qs_ref[...], 1, 0) * SCALE
    dq = dot(keys, dscore, 0, 0)
    return dq, dk, dv


def both(ref):
    keys = jnp.concatenate([ref[:D], ref[2 * D : 3 * D]], axis=0)
    values = jnp.concatenate([ref[D : 2 * D], ref[3 * D :]], axis=0)
    return keys, values


def head_parts(out, grad):
    product = out.astype(F32) * grad.astype(F32)
    high = product.astype(BF)
    return high, (product - high.astype(F32)).astype(BF)


def head_ones(shape, axis):
    position = lax.broadcasted_iota(jnp.int32, shape, 1 - axis) // D
    return jnp.where(position == lax.broadcasted_iota(jnp.int32, shape, axis), 1.0, 0.0).astype(BF)


def stack_heads(source, target, heads, first):
    for j in range(heads):
        at = first + j * D
        target[j * D : (j + 1) * D, :] = source[:, at : at + D]


def spread_rows(rows, target, heads):
    for j in range(heads):
        target[:, j * D : (j + 1) * D] = rows[j : j + 1, :]


def unstack_query_grad(dq, heads):
    dq = (dq * SCALE).astype(BF)
    return [dq[:, j * D : (j + 1) * D].T for j in range(heads)]


def pack_kernel(heads, groups, total, len_hbm, do_ref, o_ref, q_ref, k_ref, v_ref, ex_ref, dk_ref, dv_ref, pay_ref, kv_ref, *refs):
    grad, out, query, keys, values, buf, len_ref, block, high, low, sems = refs
    rows = out.shape[0]
    wide = heads * D
    pairs = (
        (do_ref, grad), (o_ref, out), (q_ref, query), (k_ref, keys), (v_ref, values), (ex_ref, buf), (len_hbm, len_ref),
        (dk_ref, kv_ref.at[pl.ds(0, D)]), (dv_ref, kv_ref.at[pl.ds(D, D)]),
    )
    loads = [pltpu.make_async_copy(source, to, sems.at[n]) for n, (source, to) in enumerate(pairs)]
    for load in loads:
        load.start()
    sends = []

    def send(to, size):
        cut = (slice(None), slice(None), pl.ds(to, size))
        sends.append(pltpu.make_async_copy(block.at[cut], pay_ref.at[cut], sems.at[len(pairs) + len(sends)]))
        sends[-1].start()

    def place(source, to, size):
        for g in range(groups):
            block[g, :, to : to + size] = source[:, g * size : (g + 1) * size]

    loads[0].wait()
    place(grad, wide, wide)
    send(wide, wide)
    loads[2].wait()
    place(query, 0, wide)
    send(0, wide)
    loads[1].wait()
    for g in range(groups):
        cut, at = slice(g * wide, (g + 1) * wide), slice(g * rows, (g + 1) * rows)
        high[at, :], low[at, :] = head_parts(out[:, cut], grad[:, cut])
    ones = head_ones((wide, D), 1)
    deltas = dot(high[...], ones, 1, 0) + dot(low[...], ones, 1, 0)
    loads[5].wait()
    loads[6].wait()
    row = lax.axis_index("head") * rows + sublanes((rows, D))
    within = jnp.where(row < len_ref[0, 0], row, row - len_ref[0, 0])
    log_count = jnp.log((within + 1 + total).astype(F32))
    lse = (buf[...] + log_count[:, : heads * groups]) * LOG2E
    lse = jnp.concatenate([lse, jnp.zeros((rows, D - heads * groups), F32)], axis=1)
    lane = lanes((rows, D))
    for g in range(groups):
        mine = lse if g == 0 else pltpu.roll(lse, D - heads * g, 1)
        mine = jnp.where(lane < heads, mine, 0.0)
        stats = jnp.zeros((rows, D), F32)
        for n, value in enumerate((mine, deltas[g * rows : (g + 1) * rows])):
            for m in range(3):
                part = value.astype(BF).astype(F32)
                value = value - part
                at = (3 * n + m) * 16
                stats = stats + (pltpu.roll(part, at, 1) if at else part)
        block[g, :, 2 * wide + 2 * D :] = jnp.where(lane == 96, (row - within).astype(F32), stats).astype(BF)
    loads[3].wait()
    loads[4].wait()
    place(keys, 2 * wide, D)
    place(values, 2 * wide + D, D)
    send(2 * wide, 3 * D)
    for copy in loads[7:] + sends:
        copy.wait()


def doc_keys(order_ref, me, ctx_size, piece):
    core, z = piece
    place, low, step = me // 4, (me // 2) % 2, ctx_size // 4
    depth = lax.rem(place + z, step)
    return [(depth * 2 + (low ^ x if isinstance(low, int) else lax.bitwise_xor(low, x))) * 2 + lax.bitwise_xor(lax.rem(me, 2), core) for x in range(2)]


def doc_lse(order_ref, me, owner, lse, lane_half):
    parts = []
    for b in range(2):
        kb = order_ref[2 * owner + b]
        bias = [jnp.where(kb <= order_ref[2 * me + a], 0.0, HIDDEN).astype(F32) for a in range(2)]
        parts.append(lse + jnp.where(lane_half, bias[1], bias[0]))
    return parts


def doc_kernel(core, heads, ctx_size, order_ref, *refs):
    kv_refs, refs = refs[:4], refs[4:]
    stores = []

    def store(source, to):
        stores.append(pltpu.make_async_copy(source, to, sems.at[len(stores)]))
        stores[-1].start()

    if core == 0:
        q_ref, o_ref, do_ref, ex_ref, *state, dq_ref, near_ref, own_ref = refs
    else:
        *state, dq_in, near_ref, own_ref, far_hbm, dq_hbm, near_hbm, own_hbm, far_ref, dq_ref, sems = refs
        store(near_ref, near_hbm)
        store(own_ref, own_hbm)
    qs_ref, dos_ref, lse_ref, delta_ref = state

    me = lax.axis_index("ctx")
    rows = heads * D
    lane = lax.rem(lanes((1, rows)), D)
    half = D // 2
    lane_half = lane >= half
    if core == 0:
        one = lanes((1, D))
        pos = jnp.where(one < half, order_ref[2 * me] * half + one, order_ref[2 * me + 1] * half + one - half)
        spread_rows((ex_ref[...] + jnp.log((pos + 1).astype(F32))) * LOG2E, lse_ref, heads)
        stack_heads(q_ref, qs_ref, heads, 0)
        stack_heads(do_ref, dos_ref, heads, 0)
        ones = head_ones((16, rows), 0)
        high, low = head_parts(o_ref[...], do_ref[...])
        spread_rows(dot(ones, high, 1, 1) + dot(ones, low, 1, 1), delta_ref, heads)
    lse = lse_ref[...]
    delta = delta_ref[...]
    total = None
    for depth in range(4):
        owners = doc_keys(order_ref, me, ctx_size, (core, depth))
        shift = [row for o in owners for row in doc_lse(order_ref, me, o, lse, lane_half)]
        mask = None
        if core == 0 and depth == 0:
            key = sublanes((2 * D, 1))
            key_pos = jnp.where(key < half, order_ref[2 * me] * half + key, order_ref[2 * me + 1] * half + key - half)
            row_pos = jnp.where(lane_half, order_ref[2 * me + 1] * half + lane - half, order_ref[2 * me] * half + lane)
            mask = jnp.where(key < D, key_pos, -1) <= row_pos
        dq, dk, dv = pair_block(qs_ref, dos_ref, *both(kv_refs[depth]), shift, delta, mask)
        for side, grad in enumerate((dk, dv)):
            cut = slice(side * D, (side + 1) * D)
            if core == 0:
                own_ref[depth, :, cut] = grad[:D]
                near_ref[depth, :, cut] = grad[D:]
            else:
                far_ref[depth, :, cut] = grad.astype(BF)
        total = dq if total is None else total + dq
        if core == 1 and depth % 2 == 1:
            done = pl.ds(depth - 1, 2)
            store(far_ref.at[done], far_hbm.at[done])
    if core == 0:
        dq_ref[...] = total
    else:
        dq_ref[...] = ((total + dq_in[...]) * SCALE).astype(BF)
        store(dq_ref, dq_hbm)
    for copy in stores:
        copy.wait()


def turn_kernel(heads, turned_ref, out_ref):
    for j in range(heads):
        out_ref[:, j * D : (j + 1) * D] = turned_ref[:, j * D : (j + 1) * D].T


def far_kernel(heads, pay_ref, *refs):
    kv_refs, (send_ref, dq_ref, qs_ref, dos_ref, lse_ref, delta_ref) = refs[:4], refs[4:]
    wide = heads * D
    stack_heads(pay_ref, qs_ref, heads, 0)
    stack_heads(pay_ref, dos_ref, heads, wide)
    stats = pay_ref[:, 2 * wide + 2 * D :].astype(F32).T
    spread_rows(stats[:16] + stats[16:32] + stats[32:48], lse_ref, heads)
    spread_rows(stats[48:64] + stats[64:80] + stats[80:96], delta_ref, heads)
    lse, delta = lse_ref[...], delta_ref[...]
    total = None
    for n in range(4):
        dq, dk, dv = pair_block(qs_ref, dos_ref, *both(kv_refs[n]), lse, delta, None)
        send_ref[n, :, :D] = dk.astype(BF)
        send_ref[n, :, D:] = dv.astype(BF)
        total = dq if total is None else total + dq
    dq_ref[...] = total


def column(x, qs_ref, dos_ref, lse, delta, kv_refs, total, store):
    for pair in range(len(kv_refs) // 2):
        refs = [kv_refs[2 * pair + m] for m in range(2)]
        keys = jnp.concatenate([ref[2 * x * D : 2 * x * D + D] for ref in refs], axis=0)
        values = jnp.concatenate([ref[2 * x * D + D : 2 * x * D + 2 * D] for ref in refs], axis=0)
        dq, dk, dv = pair_block(qs_ref, dos_ref, keys, values, lse, delta, None)
        for m in range(2):
            part = slice(m * D, (m + 1) * D)
            store(2 * pair + m, slice(0, D), dk[part])
            store(2 * pair + m, slice(D, 2 * D), dv[part])
        total = total + dq
    return total


def near_kernel(qs_ref, dos_ref, lse_ref, delta_ref, dq_in, core_ref, core_doc_ref, *refs):
    kv_refs, doc_ref = refs[:4], refs[4]
    send_ref, dq_ref = refs[5:]

    def store(n, cut, grad):
        send_ref[n, :, cut] = (grad + doc_ref[n, :, cut] + core_ref[n, D:, cut].astype(F32) + core_doc_ref[n, D:, cut].astype(F32)).astype(BF)

    dq_ref[...] = column(1, qs_ref, dos_ref, lse_ref[...], delta_ref[...], kv_refs, dq_in[...], store)


def own_kernel(heads, qs_ref, dos_ref, lse_ref, delta_ref, dq_in, pay_ref, *refs):
    kv_refs = refs[:2]
    out_ref, self_ref, dq_ref = refs[2:]
    wide = heads * D
    lse, delta = lse_ref[...], delta_ref[...]
    stats = pay_ref[:, 2 * wide + 2 * D :].astype(F32).T
    row = lanes((1, D))
    key = sublanes((D, 1))
    seen = (key <= row) & (key >= stats[96:97].astype(jnp.int32))
    mask = jnp.concatenate([seen] * heads, axis=1)
    keys = pay_ref[:, 2 * wide : 2 * wide + D]
    values = pay_ref[:, 2 * wide + D : 2 * wide + 2 * D]
    dq, dk, dv = pair_block(qs_ref, dos_ref, keys, values, lse, delta, mask)
    self_ref[:, :D] = dk.astype(BF)
    self_ref[:, D:] = dv.astype(BF)

    def store(n, cut, grad):
        out_ref[n, :, cut] = grad

    dq_ref[...] = column(0, qs_ref, dos_ref, lse, delta, kv_refs, dq_in[...] + dq, store)


def last_kernel(heads, groups, qs_ref, dos_ref, lse_ref, delta_ref, dq_in, self_ref, low_ref, core_ref, core_doc_ref, doc_ref, *refs):
    kv_refs = refs[:2]
    out_ref, back_hbm, back_ref, sems = refs[2:]
    wide = heads * D
    each = D // groups
    copies = []

    def send(at, size):
        cut = (slice(None), slice(None), pl.ds(at, size))
        copies.append(pltpu.make_async_copy(back_ref.at[cut], back_hbm.at[cut], sems.at[len(copies)]))
        copies[-1].start()

    for g in range(groups):
        back_ref[g, :, wide:] = self_ref[g * each : (g + 1) * each]
    send(wide, 2 * D)

    def other(n, cut):
        return doc_ref[n, :, cut] + core_ref[n, :D, cut].astype(F32) + core_doc_ref[n, :D, cut].astype(F32)

    def store(n, cut, grad):
        out_ref[n + 2, :, cut] = grad + other(n + 2, cut)

    total = column(0, qs_ref, dos_ref, lse_ref[...], delta_ref[...], kv_refs, dq_in[...], store)
    for j, part in enumerate(unstack_query_grad(total, heads)):
        for g in range(groups):
            back_ref[g, :, j * D : (j + 1) * D] = part[g * each : (g + 1) * each]
        if j % 4 == 3:
            send((j - 3) * D, 4 * D)
    for n in range(2):
        out_ref[n] = low_ref[n] + other(n, slice(0, 2 * D))
    for copy in copies:
        copy.wait()


def held_kernel(own_ref, chip_ref, keep_ref, *send_refs):
    for n in range(4):
        held = own_ref[n] + chip_ref[n].astype(F32)
        if n == 0:
            keep_ref[...] = held
        else:
            send_refs[n - 1][...] = held.astype(BF)


def unpack_kernel(heads, groups, back_ref, keep_ref, *refs):
    q_ref, k_ref, v_ref, dk_ref, dv_ref = refs[3:]
    wide = heads * D
    total = keep_ref[...]
    for ref in refs[:3]:
        total = total + ref[...].astype(F32)
    dk_ref[...] = total[:, :D].astype(BF)
    dv_ref[...] = total[:, D:].astype(BF)
    for g in range(groups):
        q_ref[:, g * wide : (g + 1) * wide] = back_ref[g, :, :wide]
        k_ref[:, g * D : (g + 1) * D] = back_ref[g, :, wide : wide + D]
        v_ref[:, g * D : (g + 1) * D] = back_ref[g, :, wide + D :]


def local(
    block_order,
    question_lengths,
    document_query_matrix,
    document_key_matrix,
    document_value_matrix,
    document_output,
    document_outgrad,
    document_excess,
    question_query_matrix,
    question_key_matrix,
    question_value_matrix,
    question_output,
    question_outgrad,
    question_excess,
):
    ctx_size, groups = lax.axis_size("ctx"), lax.axis_size("head")
    heads = document_excess.shape[1]
    rows, each = document_query_matrix.shape[0], question_query_matrix.shape[0]
    total_doc = rows * ctx_size
    wide, stacked = heads * D, heads * rows
    depth = ctx_size // 4

    def other_core(x):
        return lax.ppermute(x, "ctx", [(i, i ^ 1) for i in range(ctx_size)])

    def other_chip(x):
        return lax.ppermute(x, "ctx", [(i, i ^ 2) for i in range(ctx_size)])

    def along_z(x, d):
        return lax.ppermute(x, "ctx", [(i, (i + 4 * d) % ctx_size) for i in range(ctx_size)])

    chip = [other_chip(document_key_matrix), other_chip(document_value_matrix)]
    asking = pltpu.VMEM((each, wide * groups), BF)
    narrow = pltpu.VMEM((each, D * groups), BF)
    both_parts = pltpu.VMEM((groups * each, wide), BF)
    payload, kv = pl.pallas_call(
        functools.partial(pack_kernel, heads, groups, total_doc),
        out_shape=(
            pltpu.HBM((groups, each, 2 * wide + 3 * D), BF),
            jax.ShapeDtypeStruct((4 * rows, D), BF),
        ),
        in_specs=[hbm()] * 9,
        out_specs=(hbm(), vmem()),
        scratch_shapes=[asking, asking, asking, narrow, narrow, pltpu.VMEM((each, heads * groups), F32)]
        + [pltpu.SMEM(question_lengths.shape, jnp.int32), pltpu.VMEM((groups, each, 2 * wide + 3 * D), BF), both_parts, both_parts]
        + [pltpu.SemaphoreType.DMA((12,))],
        compiler_params=SHARED,
        cost_estimate=cost(5),
    )(
        *[
            pltpu.with_memory_space_constraint(x, pltpu.HBM)
            for x in (
                question_lengths, question_outgrad, question_output, question_query_matrix, question_key_matrix,
                question_value_matrix, question_excess, document_key_matrix, document_value_matrix,
            )
        ],
    )
    here = kv
    for n, part in enumerate(chip):
        here = lax.dynamic_update_slice(here, part, ((2 + n) * rows, 0))
    mine = [here] + [along_z(here, depth - d) for d in range(1, depth)]
    theirs = [other_core(piece) for piece in mine]
    asked = lax.all_to_all(payload, "head", 0, 0, tiled=True).reshape(groups * each, -1)

    quarter = ((depth, rows, 2 * D), F32)
    double = ((depth, 2 * rows, 2 * D), BF)
    row_state = [((stacked, D), BF), ((stacked, D), BF), ((1, stacked), F32), ((1, stacked), F32)]
    query_sum = ((D, stacked), F32)
    flat = ((rows, wide), BF)

    *doc_state, dq, near_doc, own_doc = call(
        6,
        functools.partial(doc_kernel, 0, heads, ctx_size),
        row_state + [query_sum, quarter, quarter],
        1,
        block_order, *mine, document_query_matrix, document_output, document_outgrad, document_excess.T,
    )
    turned = ((D, stacked), BF)
    far_doc, doc_turned, near_doc, own_doc = pl.pallas_call(
        functools.partial(doc_kernel, 1, heads, ctx_size),
        out_shape=tuple(pltpu.HBM(*out) for out in (double, turned, quarter, quarter)),
        in_specs=[smem()] + [vmem()] * 11,
        out_specs=(hbm(),) * 4,
        scratch_shapes=[pltpu.VMEM(*double), pltpu.VMEM(*turned), pltpu.SemaphoreType.DMA((5,))],
        compiler_params=SHARED,
        cost_estimate=cost(6),
    )(block_order, *theirs, *doc_state, dq, near_doc, own_doc)
    core_doc = other_core(far_doc)
    far, dq, *state = call(
        4.8, functools.partial(far_kernel, heads), [double, query_sum] + row_state, 0, asked, *theirs
    )
    core_sum = other_core(far)
    low, own_self, dq = call(
        2,
        functools.partial(own_kernel, heads),
        [((2, rows, 2 * D), F32), ((rows, 2 * D), BF), query_sum],
        0,
        *state, dq, asked, *mine[:2],
    )
    near, dq = call(2.2, near_kernel, [((depth, rows, 2 * D), BF), query_sum], 0, *state, dq, core_sum, core_doc, *mine, near_doc)
    chip_sum = other_chip(near)
    returned = ((groups, each, wide + 2 * D), BF)
    own, back = pl.pallas_call(
        functools.partial(last_kernel, heads, groups),
        out_shape=(jax.ShapeDtypeStruct(*quarter), pltpu.HBM(*returned)),
        in_specs=[vmem()] * 12,
        out_specs=(vmem(), hbm()),
        scratch_shapes=[pltpu.VMEM(*returned), pltpu.SemaphoreType.DMA((4,))],
        compiler_params=SHARED,
        cost_estimate=cost(2),
    )(*state, dq, own_self, low, core_sum, core_doc, own_doc, *mine[2:])
    back = lax.all_to_all(back, "head", 0, 0, tiled=True)
    keep, *sends = call(
        25,
        held_kernel,
        [((rows, 2 * D), F32)] + [((rows, 2 * D), BF)] * (depth - 1),
        0,
        own, chip_sum,
    )
    (document_query_grad,) = call(2, functools.partial(turn_kernel, heads), [flat], 0, doc_turned)
    arrived = [along_z(send, n + 1) for n, send in enumerate(sends)]
    question_query_grad, question_keys_grad, question_values_grad, document_keys_grad, document_values_grad = call(
        0.8,
        functools.partial(unpack_kernel, heads, groups),
        [((each, wide * groups), BF), ((each, D * groups), BF), ((each, D * groups), BF), ((rows, D), BF), ((rows, D), BF)],
        0,
        back, keep, *arrived,
    )
    return (
        document_query_grad,
        document_keys_grad,
        document_values_grad,
        question_query_grad,
        question_keys_grad,
        question_values_grad,
    )


def solution(mesh):
    return jax.shard_map(
        local,
        mesh=mesh,
        in_specs=(
            P(),
            P("ctx", None),
            P("ctx", "head"),
            P("ctx", "head"),
            P("ctx", "head"),
            P("ctx", "head"),
            P("ctx", "head"),
            P("ctx", "head"),
            P(("ctx", "head"), None),
            P(("ctx", "head"), None),
            P(("ctx", "head"), None),
            P(("ctx", "head"), None),
            P(("ctx", "head"), None),
            P(("ctx", "head"), None),
        ),
        out_specs=(
            P("ctx", "head"),
            P("ctx", "head"),
            P("ctx", "head"),
            P(("ctx", "head"), None),
            P(("ctx", "head"), None),
            P(("ctx", "head"), None),
        ),
        check_vma=False,
    )
```

```python
import functools

import jax
import jax.numpy as jnp
from jax import lax
from jax.experimental import pallas as pl
from jax.experimental.pallas import tpu as pltpu
from jax.sharding import PartitionSpec as P

D = 128
SCALE = D**-0.5
LOG2E = 1.4426950408889634
HIDDEN = 1e30
BF = jnp.bfloat16
F32 = jnp.float32
SHARED = pltpu.CompilerParams(vmem_limit_bytes=20 * 2**20)
WHOLE = pltpu.CompilerParams(vmem_limit_bytes=60 * 2**20)


def dot(a, b, ca, cb):
    return lax.dot_general(a, b, (((ca,), (cb,)), ((), ())), preferred_element_type=F32)


def lanes(shape):
    return lax.broadcasted_iota(jnp.int32, shape, 1)


def sublanes(shape):
    return lax.broadcasted_iota(jnp.int32, shape, 0)


def smem():
    return pl.BlockSpec(memory_space=pltpu.SMEM)


def vmem():
    return pl.BlockSpec(memory_space=pltpu.VMEM)


def hbm():
    return pl.BlockSpec(memory_space=pltpu.HBM)


def cost(us):
    return pl.CostEstimate(flops=int(us * 1.1e9), bytes_accessed=0, transcendentals=0)


def call(us, body, outs, n_smem, *args, **kw):
    return pl.pallas_call(
        body,
        out_shape=tuple(jax.ShapeDtypeStruct(s, t) for s, t in outs),
        in_specs=[smem()] * n_smem + [vmem()] * (len(args) - n_smem),
        out_specs=tuple(vmem() for _ in outs),
        compiler_params=SHARED,
        cost_estimate=cost(us),
        **kw,
    )(*args)


def pair_block(qs_ref, dos_ref, keys, values, lse, delta, mask):
    scores = dot(keys, qs_ref[...], 1, 1)
    dprob = dot(values, dos_ref[...], 1, 1)
    scores = scores * (SCALE * LOG2E)
    if isinstance(lse, list):
        step = scores.shape[0] // len(lse)
        prob = jnp.concatenate([jnp.exp2(scores[n * step : (n + 1) * step] - row) for n, row in enumerate(lse)], axis=0)
    else:
        prob = jnp.exp2(scores - lse)
    if mask is not None:
        prob = jnp.where(mask, prob, 0.0)
    dscore = (prob * (dprob - delta)).astype(BF)
    dv = dot(prob.astype(BF), dos_ref[...], 1, 0)
    dk = dot(dscore, qs_ref[...], 1, 0) * SCALE
    return (keys, dscore), dk, dv


def spread(blocks):
    keys, dscore = (jnp.concatenate(part, axis=0) for part in zip(*blocks))
    return dot(keys, dscore, 0, 0)


def both(ref):
    keys = jnp.concatenate([ref[:D], ref[2 * D : 3 * D]], axis=0)
    values = jnp.concatenate([ref[D : 2 * D], ref[3 * D :]], axis=0)
    return keys, values


def head_parts(out, grad):
    product = out.astype(F32) * grad.astype(F32)
    high = product.astype(BF)
    return high, (product - high.astype(F32)).astype(BF)


def head_ones(shape, axis):
    position = lax.broadcasted_iota(jnp.int32, shape, 1 - axis) // D
    return jnp.where(position == lax.broadcasted_iota(jnp.int32, shape, axis), 1.0, 0.0).astype(BF)


def stack_heads(source, target, heads, first):
    for j in range(heads):
        at = first + j * D
        target[j * D : (j + 1) * D, :] = source[:, at : at + D]


def spread_rows(rows, target, heads):
    for j in range(heads):
        target[:, j * D : (j + 1) * D] = rows[j : j + 1, :]


def unstack_query_grad(dq, heads):
    dq = (dq * SCALE).astype(BF)
    return [dq[:, j * D : (j + 1) * D].T for j in range(heads)]


def pack_kernel(heads, groups, total, len_hbm, do_ref, o_ref, q_ref, k_ref, v_ref, ex_ref, dk_ref, dv_ref, pay_ref, kv_ref, *refs):
    grad, out, query, keys, values, buf, len_ref, block, high, low, sems = refs
    rows = out.shape[0]
    wide = heads * D
    pairs = (
        (do_ref, grad), (o_ref, out), (q_ref, query), (k_ref, keys), (v_ref, values), (ex_ref, buf), (len_hbm, len_ref),
        (dk_ref, kv_ref.at[pl.ds(0, D)]), (dv_ref, kv_ref.at[pl.ds(D, D)]),
    )
    loads = [pltpu.make_async_copy(source, to, sems.at[n]) for n, (source, to) in enumerate(pairs)]
    for load in loads:
        load.start()
    sends = []

    def send(to, size):
        cut = (slice(None), slice(None), pl.ds(to, size))
        sends.append(pltpu.make_async_copy(block.at[cut], pay_ref.at[cut], sems.at[len(pairs) + len(sends)]))
        sends[-1].start()

    def place(source, to, size):
        for g in range(groups):
            block[g, :, to : to + size] = source[:, g * size : (g + 1) * size]

    loads[0].wait()
    place(grad, wide, wide)
    send(wide, wide)
    loads[2].wait()
    place(query, 0, wide)
    send(0, wide)
    loads[1].wait()
    for g in range(groups):
        cut, at = slice(g * wide, (g + 1) * wide), slice(g * rows, (g + 1) * rows)
        high[at, :], low[at, :] = head_parts(out[:, cut], grad[:, cut])
    ones = head_ones((wide, D), 1)
    deltas = dot(high[...], ones, 1, 0) + dot(low[...], ones, 1, 0)
    loads[5].wait()
    loads[6].wait()
    row = lax.axis_index("head") * rows + sublanes((rows, D))
    within = jnp.where(row < len_ref[0, 0], row, row - len_ref[0, 0])
    log_count = jnp.log((within + 1 + total).astype(F32))
    lse = (buf[...] + log_count[:, : heads * groups]) * LOG2E
    lse = jnp.concatenate([lse, jnp.zeros((rows, D - heads * groups), F32)], axis=1)
    lane = lanes((rows, D))
    for g in range(groups):
        mine = lse if g == 0 else pltpu.roll(lse, D - heads * g, 1)
        mine = jnp.where(lane < heads, mine, 0.0)
        stats = jnp.zeros((rows, D), F32)
        for n, value in enumerate((mine, deltas[g * rows : (g + 1) * rows])):
            for m in range(3):
                part = value.astype(BF).astype(F32)
                value = value - part
                at = (3 * n + m) * 16
                stats = stats + (pltpu.roll(part, at, 1) if at else part)
        block[g, :, 2 * wide + 2 * D :] = jnp.where(lane == 96, (row - within).astype(F32), stats).astype(BF)
    loads[3].wait()
    loads[4].wait()
    place(keys, 2 * wide, D)
    place(values, 2 * wide + D, D)
    send(2 * wide, 3 * D)
    for copy in loads[7:] + sends:
        copy.wait()


def doc_keys(order_ref, me, ctx_size, piece):
    core, z = piece
    place, low, step = me // 4, (me // 2) % 2, ctx_size // 4
    depth = lax.rem(place + z, step)
    return [(depth * 2 + (low ^ x if isinstance(low, int) else lax.bitwise_xor(low, x))) * 2 + lax.bitwise_xor(lax.rem(me, 2), core) for x in range(2)]


def doc_lse(order_ref, me, owner, lse, lane_half):
    parts = []
    for b in range(2):
        kb = order_ref[2 * owner + b]
        bias = [jnp.where(kb <= order_ref[2 * me + a], 0.0, HIDDEN).astype(F32) for a in range(2)]
        parts.append(lse + jnp.where(lane_half, bias[1], bias[0]))
    return parts


def doc_kernel(core, heads, ctx_size, order_ref, *refs):
    kv_refs, refs = refs[:4], refs[4:]
    stores = []

    def store(source, to):
        stores.append(pltpu.make_async_copy(source, to, sems.at[len(stores)]))
        stores[-1].start()

    if core == 0:
        q_ref, o_ref, do_ref, ex_ref, *state, dq_ref, near_ref, own_ref = refs
    else:
        *state, dq_in, near_ref, own_ref, far_ref, dq_ref, near_hbm, own_hbm, sems = refs
        store(near_ref, near_hbm)
        store(own_ref, own_hbm)
    qs_ref, dos_ref, lse_ref, delta_ref = state

    me = lax.axis_index("ctx")
    rows = heads * D
    lane = lax.rem(lanes((1, rows)), D)
    half = D // 2
    lane_half = lane >= half
    if core == 0:
        one = lanes((1, D))
        pos = jnp.where(one < half, order_ref[2 * me] * half + one, order_ref[2 * me + 1] * half + one - half)
        spread_rows((ex_ref[...] + jnp.log((pos + 1).astype(F32))) * LOG2E, lse_ref, heads)
        stack_heads(q_ref, qs_ref, heads, 0)
        stack_heads(do_ref, dos_ref, heads, 0)
        ones = head_ones((16, rows), 0)
        high, low = head_parts(o_ref[...], do_ref[...])
        spread_rows(dot(ones, high, 1, 1) + dot(ones, low, 1, 1), delta_ref, heads)
    lse = lse_ref[...]
    delta = delta_ref[...]
    total, blocks = None, []
    for depth in range(4):
        owners = doc_keys(order_ref, me, ctx_size, (core, depth))
        shift = [row for o in owners for row in doc_lse(order_ref, me, o, lse, lane_half)]
        mask = None
        if core == 0 and depth == 0:
            key = sublanes((2 * D, 1))
            key_pos = jnp.where(key < half, order_ref[2 * me] * half + key, order_ref[2 * me + 1] * half + key - half)
            row_pos = jnp.where(lane_half, order_ref[2 * me + 1] * half + lane - half, order_ref[2 * me] * half + lane)
            mask = jnp.where(key < D, key_pos, -1) <= row_pos
        block, dk, dv = pair_block(qs_ref, dos_ref, *both(kv_refs[depth]), shift, delta, mask)
        blocks.append(block)
        for side, grad in enumerate((dk, dv)):
            cut = slice(side * D, (side + 1) * D)
            if core == 0:
                own_ref[depth, :, cut] = grad[:D]
                near_ref[depth, :, cut] = grad[D:]
            else:
                far_ref[depth, :, cut] = grad.astype(BF)
        if len(blocks) == 2:
            dq, blocks = spread(blocks), []
            total = dq if total is None else total + dq
    if core == 0:
        dq_ref[...] = total
    else:
        dq_ref[...] = ((total + dq_in[...]) * SCALE).astype(BF)
    for copy in stores:
        copy.wait()


def turn_kernel(heads, turned_ref, out_ref):
    for j in range(heads):
        out_ref[:, j * D : (j + 1) * D] = turned_ref[:, j * D : (j + 1) * D].T


def far_kernel(heads, pay_ref, *refs):
    kv_refs, (send_ref, dq_ref, qs_ref, dos_ref, lse_ref, delta_ref) = refs[:4], refs[4:]
    wide = heads * D
    stack_heads(pay_ref, qs_ref, heads, 0)
    stack_heads(pay_ref, dos_ref, heads, wide)
    stats = pay_ref[:, 2 * wide + 2 * D :].astype(F32).T
    spread_rows(stats[:16] + stats[16:32] + stats[32:48], lse_ref, heads)
    spread_rows(stats[48:64] + stats[64:80] + stats[80:96], delta_ref, heads)
    lse, delta = lse_ref[...], delta_ref[...]
    total, blocks = None, []
    for n in range(4):
        block, dk, dv = pair_block(qs_ref, dos_ref, *both(kv_refs[n]), lse, delta, None)
        send_ref[n, :, :D] = dk.astype(BF)
        send_ref[n, :, D:] = dv.astype(BF)
        blocks.append(block)
        if len(blocks) == 2:
            dq, blocks = spread(blocks), []
            total = dq if total is None else total + dq
    dq_ref[...] = total


def column(x, qs_ref, dos_ref, lse, delta, kv_refs, total, store, blocks=()):
    blocks = list(blocks)
    for pair in range(len(kv_refs) // 2):
        refs = [kv_refs[2 * pair + m] for m in range(2)]
        keys = jnp.concatenate([ref[2 * x * D : 2 * x * D + D] for ref in refs], axis=0)
        values = jnp.concatenate([ref[2 * x * D + D : 2 * x * D + 2 * D] for ref in refs], axis=0)
        block, dk, dv = pair_block(qs_ref, dos_ref, keys, values, lse, delta, None)
        for m in range(2):
            part = slice(m * D, (m + 1) * D)
            store(2 * pair + m, slice(0, D), dk[part])
            store(2 * pair + m, slice(D, 2 * D), dv[part])
        blocks.append(block)
    return total + spread(blocks)


def near_kernel(qs_ref, dos_ref, lse_ref, delta_ref, dq_in, core_ref, core_doc_ref, *refs):
    kv_refs, doc_ref = refs[:4], refs[4]
    send_ref, dq_ref = refs[5:]

    def store(n, cut, grad):
        send_ref[n, :, cut] = (grad + doc_ref[n, :, cut] + core_ref[n, D:, cut].astype(F32) + core_doc_ref[n, D:, cut].astype(F32)).astype(BF)

    dq_ref[...] = column(1, qs_ref, dos_ref, lse_ref[...], delta_ref[...], kv_refs, dq_in[...], store)


def own_kernel(heads, qs_ref, dos_ref, lse_ref, delta_ref, dq_in, pay_ref, *refs):
    kv_refs = refs[:2]
    out_ref, self_ref, dq_ref = refs[2:]
    wide = heads * D
    lse, delta = lse_ref[...], delta_ref[...]
    stats = pay_ref[:, 2 * wide + 2 * D :].astype(F32).T
    row = lanes((1, D))
    key = sublanes((D, 1))
    seen = (key <= row) & (key >= stats[96:97].astype(jnp.int32))
    mask = jnp.concatenate([seen] * heads, axis=1)
    keys = pay_ref[:, 2 * wide : 2 * wide + D]
    values = pay_ref[:, 2 * wide + D : 2 * wide + 2 * D]
    block, dk, dv = pair_block(qs_ref, dos_ref, keys, values, lse, delta, mask)
    self_ref[:, :D] = dk.astype(BF)
    self_ref[:, D:] = dv.astype(BF)

    def store(n, cut, grad):
        out_ref[n, :, cut] = grad

    dq_ref[...] = column(0, qs_ref, dos_ref, lse, delta, kv_refs, dq_in[...], store, [block])


def last_kernel(heads, groups, qs_ref, dos_ref, lse_ref, delta_ref, dq_in, self_ref, low_ref, core_ref, core_doc_ref, doc_ref, *refs):
    kv_refs = refs[:2]
    out_ref, back_hbm, back_ref, sems = refs[2:]
    wide = heads * D
    each = D // groups
    copies = []

    def send(at, size):
        cut = (slice(None), slice(None), pl.ds(at, size))
        copies.append(pltpu.make_async_copy(back_ref.at[cut], back_hbm.at[cut], sems.at[len(copies)]))
        copies[-1].start()

    for g in range(groups):
        back_ref[g, :, wide:] = self_ref[g * each : (g + 1) * each]
    send(wide, 2 * D)

    def other(n, cut):
        return doc_ref[n, :, cut] + core_ref[n, :D, cut].astype(F32) + core_doc_ref[n, :D, cut].astype(F32)

    def store(n, cut, grad):
        out_ref[n + 2, :, cut] = grad + other(n + 2, cut)

    total = column(0, qs_ref, dos_ref, lse_ref[...], delta_ref[...], kv_refs, dq_in[...], store)
    for j, part in enumerate(unstack_query_grad(total, heads)):
        for g in range(groups):
            back_ref[g, :, j * D : (j + 1) * D] = part[g * each : (g + 1) * each]
        if j % 4 == 3:
            send((j - 3) * D, 4 * D)
    for n in range(2):
        out_ref[n] = low_ref[n] + other(n, slice(0, 2 * D))
    for copy in copies:
        copy.wait()


def held_kernel(own_ref, chip_ref, keep_ref, *send_refs):
    for n in range(4):
        held = own_ref[n] + chip_ref[n].astype(F32)
        if n == 0:
            keep_ref[...] = held
        else:
            send_refs[n - 1][...] = held.astype(BF)


def unpack_kernel(heads, groups, back_ref, keep_ref, *refs):
    q_ref, k_ref, v_ref, dk_ref, dv_ref = refs[3:]
    wide = heads * D
    total = keep_ref[...]
    for ref in refs[:3]:
        total = total + ref[...].astype(F32)
    dk_ref[...] = total[:, :D].astype(BF)
    dv_ref[...] = total[:, D:].astype(BF)
    for g in range(groups):
        q_ref[:, g * wide : (g + 1) * wide] = back_ref[g, :, :wide]
        k_ref[:, g * D : (g + 1) * D] = back_ref[g, :, wide : wide + D]
        v_ref[:, g * D : (g + 1) * D] = back_ref[g, :, wide + D :]


def local(
    block_order,
    question_lengths,
    document_query_matrix,
    document_key_matrix,
    document_value_matrix,
    document_output,
    document_outgrad,
    document_excess,
    question_query_matrix,
    question_key_matrix,
    question_value_matrix,
    question_output,
    question_outgrad,
    question_excess,
):
    ctx_size, groups = lax.axis_size("ctx"), lax.axis_size("head")
    heads = document_excess.shape[1]
    rows, each = document_query_matrix.shape[0], question_query_matrix.shape[0]
    total_doc = rows * ctx_size
    wide, stacked = heads * D, heads * rows
    depth = ctx_size // 4

    def other_core(x):
        return lax.ppermute(x, "ctx", [(i, i ^ 1) for i in range(ctx_size)])

    def other_chip(x):
        return lax.ppermute(x, "ctx", [(i, i ^ 2) for i in range(ctx_size)])

    def along_z(x, d):
        return lax.ppermute(x, "ctx", [(i, (i + 4 * d) % ctx_size) for i in range(ctx_size)])

    chip = [other_chip(document_key_matrix), other_chip(document_value_matrix)]
    asking = pltpu.VMEM((each, wide * groups), BF)
    narrow = pltpu.VMEM((each, D * groups), BF)
    both_parts = pltpu.VMEM((groups * each, wide), BF)
    payload, kv = pl.pallas_call(
        functools.partial(pack_kernel, heads, groups, total_doc),
        out_shape=(
            pltpu.HBM((groups, each, 2 * wide + 3 * D), BF),
            jax.ShapeDtypeStruct((4 * rows, D), BF),
        ),
        in_specs=[hbm()] * 9,
        out_specs=(hbm(), vmem()),
        scratch_shapes=[asking, asking, asking, narrow, narrow, pltpu.VMEM((each, heads * groups), F32)]
        + [pltpu.SMEM(question_lengths.shape, jnp.int32), pltpu.VMEM((groups, each, 2 * wide + 3 * D), BF), both_parts, both_parts]
        + [pltpu.SemaphoreType.DMA((12,))],
        compiler_params=SHARED,
        cost_estimate=cost(5),
    )(
        *[
            pltpu.with_memory_space_constraint(x, pltpu.HBM)
            for x in (
                question_lengths, question_outgrad, question_output, question_query_matrix, question_key_matrix,
                question_value_matrix, question_excess, document_key_matrix, document_value_matrix,
            )
        ],
    )
    here = kv
    for n, part in enumerate(chip):
        here = lax.dynamic_update_slice(here, part, ((2 + n) * rows, 0))
    mine = [here] + [along_z(here, depth - d) for d in range(1, depth)]
    theirs = [other_core(piece) for piece in mine]
    asked = lax.all_to_all(payload, "head", 0, 0, tiled=True).reshape(groups * each, -1)

    quarter = ((depth, rows, 2 * D), F32)
    double = ((depth, 2 * rows, 2 * D), BF)
    row_state = [((stacked, D), BF), ((stacked, D), BF), ((1, stacked), F32), ((1, stacked), F32)]
    query_sum = ((D, stacked), F32)
    flat = ((rows, wide), BF)

    *doc_state, dq, near_doc, own_doc = call(
        6,
        functools.partial(doc_kernel, 0, heads, ctx_size),
        row_state + [query_sum, quarter, quarter],
        1,
        block_order, *mine, document_query_matrix, document_output, document_outgrad, document_excess.T,
    )
    turned = ((D, stacked), BF)
    far_doc, doc_turned, near_doc, own_doc = pl.pallas_call(
        functools.partial(doc_kernel, 1, heads, ctx_size),
        out_shape=tuple(jax.ShapeDtypeStruct(*out) for out in (double, turned))
        + tuple(pltpu.HBM(*out) for out in (quarter, quarter)),
        in_specs=[smem()] + [vmem()] * 11,
        out_specs=(vmem(), vmem(), hbm(), hbm()),
        scratch_shapes=[pltpu.SemaphoreType.DMA((2,))],
        compiler_params=SHARED,
        cost_estimate=cost(6),
    )(block_order, *theirs, *doc_state, dq, near_doc, own_doc)
    core_doc = other_core(far_doc)
    far, dq, *state = call(
        4.8, functools.partial(far_kernel, heads), [double, query_sum] + row_state, 0, asked, *theirs
    )
    core_sum = other_core(far)
    low, own_self, dq = call(
        2,
        functools.partial(own_kernel, heads),
        [((2, rows, 2 * D), F32), ((rows, 2 * D), BF), query_sum],
        0,
        *state, dq, asked, *mine[:2],
    )
    near, dq = call(2.2, near_kernel, [((depth, rows, 2 * D), BF), query_sum], 0, *state, dq, core_sum, core_doc, *mine, near_doc)
    chip_sum = other_chip(near)
    returned = ((groups, each, wide + 2 * D), BF)
    own, back = pl.pallas_call(
        functools.partial(last_kernel, heads, groups),
        out_shape=(jax.ShapeDtypeStruct(*quarter), pltpu.HBM(*returned)),
        in_specs=[vmem()] * 12,
        out_specs=(vmem(), hbm()),
        scratch_shapes=[pltpu.VMEM(*returned), pltpu.SemaphoreType.DMA((4,))],
        compiler_params=SHARED,
        cost_estimate=cost(2),
    )(*state, dq, own_self, low, core_sum, core_doc, own_doc, *mine[2:])
    back = lax.all_to_all(back, "head", 0, 0, tiled=True)
    keep, *sends = call(
        25,
        held_kernel,
        [((rows, 2 * D), F32)] + [((rows, 2 * D), BF)] * (depth - 1),
        0,
        own, chip_sum,
    )
    (document_query_grad,) = call(2, functools.partial(turn_kernel, heads), [flat], 0, doc_turned)
    arrived = [along_z(send, n + 1) for n, send in enumerate(sends)]
    question_query_grad, question_keys_grad, question_values_grad, document_keys_grad, document_values_grad = call(
        0.8,
        functools.partial(unpack_kernel, heads, groups),
        [((each, wide * groups), BF), ((each, D * groups), BF), ((each, D * groups), BF), ((rows, D), BF), ((rows, D), BF)],
        0,
        back, keep, *arrived,
    )
    return (
        document_query_grad,
        document_keys_grad,
        document_values_grad,
        question_query_grad,
        question_keys_grad,
        question_values_grad,
    )


def solution(mesh):
    return jax.shard_map(
        local,
        mesh=mesh,
        in_specs=(
            P(),
            P("ctx", None),
            P("ctx", "head"),
            P("ctx", "head"),
            P("ctx", "head"),
            P("ctx", "head"),
            P("ctx", "head"),
            P("ctx", "head"),
            P(("ctx", "head"), None),
            P(("ctx", "head"), None),
            P(("ctx", "head"), None),
            P(("ctx", "head"), None),
            P(("ctx", "head"), None),
            P(("ctx", "head"), None),
        ),
        out_specs=(
            P("ctx", "head"),
            P("ctx", "head"),
            P("ctx", "head"),
            P(("ctx", "head"), None),
            P(("ctx", "head"), None),
            P(("ctx", "head"), None),
        ),
        check_vma=False,
    )
```

```python
import functools

import jax
import jax.numpy as jnp
from jax import lax
from jax.experimental import pallas as pl
from jax.experimental.pallas import tpu as pltpu
from jax.sharding import PartitionSpec as P

D = 128
SCALE = D**-0.5
LOG2E = 1.4426950408889634
HIDDEN = 1e30
BF = jnp.bfloat16
F32 = jnp.float32
SHARED = pltpu.CompilerParams(vmem_limit_bytes=20 * 2**20)
WHOLE = pltpu.CompilerParams(vmem_limit_bytes=60 * 2**20)


def dot(a, b, ca, cb):
    return lax.dot_general(a, b, (((ca,), (cb,)), ((), ())), preferred_element_type=F32)


def lanes(shape):
    return lax.broadcasted_iota(jnp.int32, shape, 1)


def sublanes(shape):
    return lax.broadcasted_iota(jnp.int32, shape, 0)


def smem():
    return pl.BlockSpec(memory_space=pltpu.SMEM)


def vmem():
    return pl.BlockSpec(memory_space=pltpu.VMEM)


def hbm():
    return pl.BlockSpec(memory_space=pltpu.HBM)


def cost(us):
    return pl.CostEstimate(flops=int(us * 1.1e9), bytes_accessed=0, transcendentals=0)


def call(us, body, outs, n_smem, *args, **kw):
    return pl.pallas_call(
        body,
        out_shape=tuple(jax.ShapeDtypeStruct(s, t) for s, t in outs),
        in_specs=[smem()] * n_smem + [vmem()] * (len(args) - n_smem),
        out_specs=tuple(vmem() for _ in outs),
        compiler_params=SHARED,
        cost_estimate=cost(us),
        **kw,
    )(*args)


def pair_block(qs_ref, dos_ref, keys, values, lse, delta, mask):
    scores = dot(keys, qs_ref[...], 1, 1)
    dprob = dot(values, dos_ref[...], 1, 1)
    scores = scores * (SCALE * LOG2E)
    if isinstance(lse, list):
        step = scores.shape[0] // len(lse)
        prob = jnp.concatenate([jnp.exp2(scores[n * step : (n + 1) * step] - row) for n, row in enumerate(lse)], axis=0)
    else:
        prob = jnp.exp2(scores - lse)
    if mask is not None:
        prob = jnp.where(mask, prob, 0.0)
    dscore = (prob * (dprob - delta)).astype(BF)
    dv = dot(prob.astype(BF), dos_ref[...], 1, 0)
    dk = dot(dscore, qs_ref[...], 1, 0) * SCALE
    return (keys, dscore), dk, dv


def spread(blocks):
    keys, dscore = (jnp.concatenate(part, axis=0) for part in zip(*blocks))
    return dot(keys, dscore, 0, 0)


def both(ref):
    keys = jnp.concatenate([ref[:D], ref[2 * D : 3 * D]], axis=0)
    values = jnp.concatenate([ref[D : 2 * D], ref[3 * D :]], axis=0)
    return keys, values


def head_parts(out, grad):
    product = out.astype(F32) * grad.astype(F32)
    high = product.astype(BF)
    return high, (product - high.astype(F32)).astype(BF)


def head_ones(shape, axis):
    position = lax.broadcasted_iota(jnp.int32, shape, 1 - axis) // D
    return jnp.where(position == lax.broadcasted_iota(jnp.int32, shape, axis), 1.0, 0.0).astype(BF)


def stack_heads(source, target, heads, first):
    for j in range(heads):
        at = first + j * D
        target[j * D : (j + 1) * D, :] = source[:, at : at + D]


def spread_rows(rows, target, heads):
    for j in range(heads):
        target[:, j * D : (j + 1) * D] = rows[j : j + 1, :]


def unstack_query_grad(dq, heads):
    dq = (dq * SCALE).astype(BF)
    return [dq[:, j * D : (j + 1) * D].T for j in range(heads)]


def pack_kernel(heads, groups, total, len_hbm, do_ref, o_ref, q_ref, k_ref, v_ref, ex_ref, dk_ref, dv_ref, pay_ref, kv_ref, *refs):
    grad, out, query, keys, values, buf, len_ref, block, high, low, sems = refs
    rows = out.shape[0]
    wide = heads * D
    pairs = (
        (do_ref, grad), (o_ref, out), (q_ref, query), (k_ref, keys), (v_ref, values), (ex_ref, buf), (len_hbm, len_ref),
        (dk_ref, kv_ref.at[pl.ds(0, D)]), (dv_ref, kv_ref.at[pl.ds(D, D)]),
    )
    loads = [pltpu.make_async_copy(source, to, sems.at[n]) for n, (source, to) in enumerate(pairs)]
    for load in loads:
        load.start()
    sends = []

    def send(to, size):
        cut = (slice(None), slice(None), pl.ds(to, size))
        sends.append(pltpu.make_async_copy(block.at[cut], pay_ref.at[cut], sems.at[len(pairs) + len(sends)]))
        sends[-1].start()

    def place(source, to, size):
        for g in range(groups):
            block[g, :, to : to + size] = source[:, g * size : (g + 1) * size]

    loads[0].wait()
    place(grad, wide, wide)
    send(wide, wide)
    loads[2].wait()
    place(query, 0, wide)
    send(0, wide)
    loads[1].wait()
    for g in range(groups):
        cut, at = slice(g * wide, (g + 1) * wide), slice(g * rows, (g + 1) * rows)
        high[at, :], low[at, :] = head_parts(out[:, cut], grad[:, cut])
    ones = head_ones((wide, D), 1)
    deltas = dot(high[...], ones, 1, 0) + dot(low[...], ones, 1, 0)
    loads[5].wait()
    loads[6].wait()
    row = lax.axis_index("head") * rows + sublanes((rows, D))
    within = jnp.where(row < len_ref[0, 0], row, row - len_ref[0, 0])
    log_count = jnp.log((within + 1 + total).astype(F32))
    lse = (buf[...] + log_count[:, : heads * groups]) * LOG2E
    lse = jnp.concatenate([lse, jnp.zeros((rows, D - heads * groups), F32)], axis=1)
    lane = lanes((rows, D))
    for g in range(groups):
        mine = lse if g == 0 else pltpu.roll(lse, D - heads * g, 1)
        mine = jnp.where(lane < heads, mine, 0.0)
        stats = jnp.zeros((rows, D), F32)
        for n, value in enumerate((mine, deltas[g * rows : (g + 1) * rows])):
            for m in range(3):
                part = value.astype(BF).astype(F32)
                value = value - part
                at = (3 * n + m) * 16
                stats = stats + (pltpu.roll(part, at, 1) if at else part)
        block[g, :, 2 * wide + 2 * D :] = jnp.where(lane == 96, (row - within).astype(F32), stats).astype(BF)
    loads[3].wait()
    loads[4].wait()
    place(keys, 2 * wide, D)
    place(values, 2 * wide + D, D)
    send(2 * wide, 3 * D)
    for copy in loads[7:] + sends:
        copy.wait()


def doc_keys(order_ref, me, ctx_size, piece):
    core, z = piece
    place, low, step = me // 4, (me // 2) % 2, ctx_size // 4
    depth = lax.rem(place + z, step)
    return [(depth * 2 + (low ^ x if isinstance(low, int) else lax.bitwise_xor(low, x))) * 2 + lax.bitwise_xor(lax.rem(me, 2), core) for x in range(2)]


def doc_lse(order_ref, me, owner, lse, lane_half):
    parts = []
    for b in range(2):
        kb = order_ref[2 * owner + b]
        bias = [jnp.where(kb <= order_ref[2 * me + a], 0.0, HIDDEN).astype(F32) for a in range(2)]
        parts.append(lse + jnp.where(lane_half, bias[1], bias[0]))
    return parts


def doc_kernel(core, heads, ctx_size, order_ref, *refs):
    kv_refs, refs = refs[:4], refs[4:]
    stores = []

    def store(source, to):
        stores.append(pltpu.make_async_copy(source, to, sems.at[len(stores)]))
        stores[-1].start()

    if core == 0:
        q_ref, o_ref, do_ref, ex_ref, *state, dq_ref, near_ref, own_ref = refs
    else:
        *state, dq_in, near_ref, own_ref, far_ref, dq_ref, near_hbm, own_hbm, sems = refs
        store(near_ref, near_hbm)
        store(own_ref, own_hbm)
    qs_ref, dos_ref, lse_ref, delta_ref = state

    me = lax.axis_index("ctx")
    rows = heads * D
    lane = lax.rem(lanes((1, rows)), D)
    half = D // 2
    lane_half = lane >= half
    if core == 0:
        one = lanes((1, D))
        pos = jnp.where(one < half, order_ref[2 * me] * half + one, order_ref[2 * me + 1] * half + one - half)
        spread_rows((ex_ref[...] + jnp.log((pos + 1).astype(F32))) * LOG2E, lse_ref, heads)
        stack_heads(q_ref, qs_ref, heads, 0)
        stack_heads(do_ref, dos_ref, heads, 0)
        ones = head_ones((16, rows), 0)
        high, low = head_parts(o_ref[...], do_ref[...])
        spread_rows(dot(ones, high, 1, 1) + dot(ones, low, 1, 1), delta_ref, heads)
    lse = lse_ref[...]
    delta = delta_ref[...]
    total, blocks = None, []
    for depth in range(4):
        owners = doc_keys(order_ref, me, ctx_size, (core, depth))
        shift = [row for o in owners for row in doc_lse(order_ref, me, o, lse, lane_half)]
        mask = None
        if core == 0 and depth == 0:
            key = sublanes((2 * D, 1))
            key_pos = jnp.where(key < half, order_ref[2 * me] * half + key, order_ref[2 * me + 1] * half + key - half)
            row_pos = jnp.where(lane_half, order_ref[2 * me + 1] * half + lane - half, order_ref[2 * me] * half + lane)
            mask = jnp.where(key < D, key_pos, -1) <= row_pos
        block, dk, dv = pair_block(qs_ref, dos_ref, *both(kv_refs[depth]), shift, delta, mask)
        blocks.append(block)
        for side, grad in enumerate((dk, dv)):
            cut = slice(side * D, (side + 1) * D)
            if core == 0:
                own_ref[depth, :, cut] = grad[:D].astype(BF)
                near_ref[depth, :, cut] = grad[D:].astype(BF)
            else:
                far_ref[depth, :, cut] = grad.astype(BF)
        if len(blocks) == 2:
            dq, blocks = spread(blocks), []
            total = dq if total is None else total + dq
    if core == 0:
        dq_ref[...] = total
    else:
        dq_ref[...] = ((total + dq_in[...]) * SCALE).astype(BF)
    for copy in stores:
        copy.wait()


def turn_kernel(heads, turned_ref, out_ref):
    for j in range(heads):
        out_ref[:, j * D : (j + 1) * D] = turned_ref[:, j * D : (j + 1) * D].T


def far_kernel(heads, pay_ref, *refs):
    kv_refs, (send_ref, dq_ref, qs_ref, dos_ref, lse_ref, delta_ref) = refs[:4], refs[4:]
    wide = heads * D
    stack_heads(pay_ref, qs_ref, heads, 0)
    stack_heads(pay_ref, dos_ref, heads, wide)
    stats = pay_ref[:, 2 * wide + 2 * D :].astype(F32).T
    spread_rows(stats[:16] + stats[16:32] + stats[32:48], lse_ref, heads)
    spread_rows(stats[48:64] + stats[64:80] + stats[80:96], delta_ref, heads)
    lse, delta = lse_ref[...], delta_ref[...]
    total, blocks = None, []
    for n in range(4):
        block, dk, dv = pair_block(qs_ref, dos_ref, *both(kv_refs[n]), lse, delta, None)
        send_ref[n, :, :D] = dk.astype(BF)
        send_ref[n, :, D:] = dv.astype(BF)
        blocks.append(block)
        if len(blocks) == 2:
            dq, blocks = spread(blocks), []
            total = dq if total is None else total + dq
    dq_ref[...] = total


def column(x, qs_ref, dos_ref, lse, delta, kv_refs, total, store, blocks=()):
    blocks = list(blocks)
    for pair in range(len(kv_refs) // 2):
        refs = [kv_refs[2 * pair + m] for m in range(2)]
        keys = jnp.concatenate([ref[2 * x * D : 2 * x * D + D] for ref in refs], axis=0)
        values = jnp.concatenate([ref[2 * x * D + D : 2 * x * D + 2 * D] for ref in refs], axis=0)
        block, dk, dv = pair_block(qs_ref, dos_ref, keys, values, lse, delta, None)
        for m in range(2):
            part = slice(m * D, (m + 1) * D)
            store(2 * pair + m, slice(0, D), dk[part])
            store(2 * pair + m, slice(D, 2 * D), dv[part])
        blocks.append(block)
    return total + spread(blocks)


def near_kernel(qs_ref, dos_ref, lse_ref, delta_ref, dq_in, core_ref, core_doc_ref, *refs):
    kv_refs, doc_ref = refs[:4], refs[4]
    send_ref, dq_ref = refs[5:]

    def store(n, cut, grad):
        send_ref[n, :, cut] = (grad + doc_ref[n, :, cut].astype(F32) + core_ref[n, D:, cut].astype(F32) + core_doc_ref[n, D:, cut].astype(F32)).astype(BF)

    dq_ref[...] = column(1, qs_ref, dos_ref, lse_ref[...], delta_ref[...], kv_refs, dq_in[...], store)


def own_kernel(heads, qs_ref, dos_ref, lse_ref, delta_ref, dq_in, pay_ref, *refs):
    kv_refs = refs[:2]
    out_ref, self_ref, dq_ref = refs[2:]
    wide = heads * D
    lse, delta = lse_ref[...], delta_ref[...]
    stats = pay_ref[:, 2 * wide + 2 * D :].astype(F32).T
    row = lanes((1, D))
    key = sublanes((D, 1))
    seen = (key <= row) & (key >= stats[96:97].astype(jnp.int32))
    mask = jnp.concatenate([seen] * heads, axis=1)
    keys = pay_ref[:, 2 * wide : 2 * wide + D]
    values = pay_ref[:, 2 * wide + D : 2 * wide + 2 * D]
    block, dk, dv = pair_block(qs_ref, dos_ref, keys, values, lse, delta, mask)
    self_ref[:, :D] = dk.astype(BF)
    self_ref[:, D:] = dv.astype(BF)

    def store(n, cut, grad):
        out_ref[n, :, cut] = grad

    dq_ref[...] = column(0, qs_ref, dos_ref, lse, delta, kv_refs, dq_in[...], store, [block])


def last_kernel(heads, groups, qs_ref, dos_ref, lse_ref, delta_ref, dq_in, self_ref, low_ref, core_ref, core_doc_ref, doc_ref, *refs):
    kv_refs = refs[:2]
    out_ref, back_hbm, back_ref, sems = refs[2:]
    wide = heads * D
    each = D // groups
    copies = []

    def send(at, size):
        cut = (slice(None), slice(None), pl.ds(at, size))
        copies.append(pltpu.make_async_copy(back_ref.at[cut], back_hbm.at[cut], sems.at[len(copies)]))
        copies[-1].start()

    for g in range(groups):
        back_ref[g, :, wide:] = self_ref[g * each : (g + 1) * each]
    send(wide, 2 * D)

    def other(n, cut):
        return doc_ref[n, :, cut].astype(F32) + core_ref[n, :D, cut].astype(F32) + core_doc_ref[n, :D, cut].astype(F32)

    def store(n, cut, grad):
        out_ref[n + 2, :, cut] = grad + other(n + 2, cut)

    total = column(0, qs_ref, dos_ref, lse_ref[...], delta_ref[...], kv_refs, dq_in[...], store)
    for j, part in enumerate(unstack_query_grad(total, heads)):
        for g in range(groups):
            back_ref[g, :, j * D : (j + 1) * D] = part[g * each : (g + 1) * each]
        if j % 4 == 3:
            send((j - 3) * D, 4 * D)
    for n in range(2):
        out_ref[n] = low_ref[n] + other(n, slice(0, 2 * D))
    for copy in copies:
        copy.wait()


def held_kernel(own_ref, chip_ref, keep_ref, *send_refs):
    for n in range(4):
        held = own_ref[n] + chip_ref[n].astype(F32)
        if n == 0:
            keep_ref[...] = held
        else:
            send_refs[n - 1][...] = held.astype(BF)


def unpack_kernel(heads, groups, back_ref, keep_ref, *refs):
    q_ref, k_ref, v_ref, dk_ref, dv_ref = refs[3:]
    wide = heads * D
    total = keep_ref[...]
    for ref in refs[:3]:
        total = total + ref[...].astype(F32)
    dk_ref[...] = total[:, :D].astype(BF)
    dv_ref[...] = total[:, D:].astype(BF)
    for g in range(groups):
        q_ref[:, g * wide : (g + 1) * wide] = back_ref[g, :, :wide]
        k_ref[:, g * D : (g + 1) * D] = back_ref[g, :, wide : wide + D]
        v_ref[:, g * D : (g + 1) * D] = back_ref[g, :, wide + D :]


def local(
    block_order,
    question_lengths,
    document_query_matrix,
    document_key_matrix,
    document_value_matrix,
    document_output,
    document_outgrad,
    document_excess,
    question_query_matrix,
    question_key_matrix,
    question_value_matrix,
    question_output,
    question_outgrad,
    question_excess,
):
    ctx_size, groups = lax.axis_size("ctx"), lax.axis_size("head")
    heads = document_excess.shape[1]
    rows, each = document_query_matrix.shape[0], question_query_matrix.shape[0]
    total_doc = rows * ctx_size
    wide, stacked = heads * D, heads * rows
    depth = ctx_size // 4

    def other_core(x):
        return lax.ppermute(x, "ctx", [(i, i ^ 1) for i in range(ctx_size)])

    def other_chip(x):
        return lax.ppermute(x, "ctx", [(i, i ^ 2) for i in range(ctx_size)])

    def along_z(x, d):
        return lax.ppermute(x, "ctx", [(i, (i + 4 * d) % ctx_size) for i in range(ctx_size)])

    chip = [other_chip(document_key_matrix), other_chip(document_value_matrix)]
    asking = pltpu.VMEM((each, wide * groups), BF)
    narrow = pltpu.VMEM((each, D * groups), BF)
    both_parts = pltpu.VMEM((groups * each, wide), BF)
    payload, kv = pl.pallas_call(
        functools.partial(pack_kernel, heads, groups, total_doc),
        out_shape=(
            pltpu.HBM((groups, each, 2 * wide + 3 * D), BF),
            jax.ShapeDtypeStruct((4 * rows, D), BF),
        ),
        in_specs=[hbm()] * 9,
        out_specs=(hbm(), vmem()),
        scratch_shapes=[asking, asking, asking, narrow, narrow, pltpu.VMEM((each, heads * groups), F32)]
        + [pltpu.SMEM(question_lengths.shape, jnp.int32), pltpu.VMEM((groups, each, 2 * wide + 3 * D), BF), both_parts, both_parts]
        + [pltpu.SemaphoreType.DMA((12,))],
        compiler_params=SHARED,
        cost_estimate=cost(5),
    )(
        *[
            pltpu.with_memory_space_constraint(x, pltpu.HBM)
            for x in (
                question_lengths, question_outgrad, question_output, question_query_matrix, question_key_matrix,
                question_value_matrix, question_excess, document_key_matrix, document_value_matrix,
            )
        ],
    )
    here = kv
    for n, part in enumerate(chip):
        here = lax.dynamic_update_slice(here, part, ((2 + n) * rows, 0))
    mine = [here] + [along_z(here, depth - d) for d in range(1, depth)]
    theirs = [other_core(piece) for piece in mine]
    asked = lax.all_to_all(payload, "head", 0, 0, tiled=True).reshape(groups * each, -1)

    quarter = ((depth, rows, 2 * D), F32)
    double = ((depth, 2 * rows, 2 * D), BF)
    single = ((depth, rows, 2 * D), BF)
    row_state = [((stacked, D), BF), ((stacked, D), BF), ((1, stacked), F32), ((1, stacked), F32)]
    query_sum = ((D, stacked), F32)
    flat = ((rows, wide), BF)

    *doc_state, dq, near_doc, own_doc = call(
        6,
        functools.partial(doc_kernel, 0, heads, ctx_size),
        row_state + [query_sum, single, single],
        1,
        block_order, *mine, document_query_matrix, document_output, document_outgrad, document_excess.T,
    )
    turned = ((D, stacked), BF)
    far_doc, doc_turned, near_doc, own_doc = pl.pallas_call(
        functools.partial(doc_kernel, 1, heads, ctx_size),
        out_shape=tuple(jax.ShapeDtypeStruct(*out) for out in (double, turned))
        + tuple(pltpu.HBM(*out) for out in (single, single)),
        in_specs=[smem()] + [vmem()] * 11,
        out_specs=(vmem(), vmem(), hbm(), hbm()),
        scratch_shapes=[pltpu.SemaphoreType.DMA((2,))],
        compiler_params=SHARED,
        cost_estimate=cost(6),
    )(block_order, *theirs, *doc_state, dq, near_doc, own_doc)
    core_doc = other_core(far_doc)
    far, dq, *state = call(
        4.8, functools.partial(far_kernel, heads), [double, query_sum] + row_state, 0, asked, *theirs
    )
    core_sum = other_core(far)
    low, own_self, dq = call(
        2,
        functools.partial(own_kernel, heads),
        [((2, rows, 2 * D), F32), ((rows, 2 * D), BF), query_sum],
        0,
        *state, dq, asked, *mine[:2],
    )
    near, dq = call(2.2, near_kernel, [((depth, rows, 2 * D), BF), query_sum], 0, *state, dq, core_sum, core_doc, *mine, near_doc)
    chip_sum = other_chip(near)
    returned = ((groups, each, wide + 2 * D), BF)
    own, back = pl.pallas_call(
        functools.partial(last_kernel, heads, groups),
        out_shape=(jax.ShapeDtypeStruct(*quarter), pltpu.HBM(*returned)),
        in_specs=[vmem()] * 12,
        out_specs=(vmem(), hbm()),
        scratch_shapes=[pltpu.VMEM(*returned), pltpu.SemaphoreType.DMA((4,))],
        compiler_params=SHARED,
        cost_estimate=cost(2),
    )(*state, dq, own_self, low, core_sum, core_doc, own_doc, *mine[2:])
    back = lax.all_to_all(back, "head", 0, 0, tiled=True)
    keep, *sends = call(
        25,
        held_kernel,
        [((rows, 2 * D), F32)] + [((rows, 2 * D), BF)] * (depth - 1),
        0,
        own, chip_sum,
    )
    (document_query_grad,) = call(2, functools.partial(turn_kernel, heads), [flat], 0, doc_turned)
    arrived = [along_z(send, n + 1) for n, send in enumerate(sends)]
    question_query_grad, question_keys_grad, question_values_grad, document_keys_grad, document_values_grad = call(
        0.8,
        functools.partial(unpack_kernel, heads, groups),
        [((each, wide * groups), BF), ((each, D * groups), BF), ((each, D * groups), BF), ((rows, D), BF), ((rows, D), BF)],
        0,
        back, keep, *arrived,
    )
    return (
        document_query_grad,
        document_keys_grad,
        document_values_grad,
        question_query_grad,
        question_keys_grad,
        question_values_grad,
    )


def solution(mesh):
    return jax.shard_map(
        local,
        mesh=mesh,
        in_specs=(
            P(),
            P("ctx", None),
            P("ctx", "head"),
            P("ctx", "head"),
            P("ctx", "head"),
            P("ctx", "head"),
            P("ctx", "head"),
            P("ctx", "head"),
            P(("ctx", "head"), None),
            P(("ctx", "head"), None),
            P(("ctx", "head"), None),
            P(("ctx", "head"), None),
            P(("ctx", "head"), None),
            P(("ctx", "head"), None),
        ),
        out_specs=(
            P("ctx", "head"),
            P("ctx", "head"),
            P("ctx", "head"),
            P(("ctx", "head"), None),
            P(("ctx", "head"), None),
            P(("ctx", "head"), None),
        ),
        check_vma=False,
    )
```
